128 devices in a mesh: seq: 16 (over y, z), ch: 8 (over x, core).
Axes of the slice: x: 4, y: 4, z: 4, core: 2. Of those that a mesh axis runs over, the one named last changes fastest.
Arguments:
- queries: bfloat16 [16384, 8192], P('seq', 'ch'), may hold values from -6 to 6
- keys: bfloat16 [16384, 8192], P('seq', 'ch'), may hold values from -6 to 6
- values: bfloat16 [16384, 8192], P('seq', 'ch'), may hold values from -6 to 6
- filters: bfloat16 [512, 128], P('ch'), may hold values from -0.5 to 0.5
- grad_out: bfloat16 [16384, 4096], P('seq', 'ch'), may hold values from -6 to 6
- out_weight: bfloat16 [4096, 8192], P('seq', 'ch'), may hold values from -0.09375 to 0.09375
Outputs:
- grad_queries: bfloat16 [16384, 8192], P('seq', 'ch')
- grad_keys: bfloat16 [16384, 8192], P('seq', 'ch')
- grad_values: bfloat16 [16384, 8192], P('seq', 'ch')
- grad_filters: float32 [512, 128], P('ch', 'seq')
- grad_weight: bfloat16 [4096, 8192], P('seq', 'ch')
The draws below stay inside these ranges and needn't reach their ends.
All inputs are finite; a program needn't handle non-finite values.
Results may differ from the reference program's by a relative error of at most 0.022.
Values may be sent and summed in bfloat16 or wider, within the bound.
A program may use at most 192 MiB of HBM per device.

```python
import jax
import jax.numpy as jnp
from jax import lax

D = 8192
FEAT_OUT = 4096
GROUP = 16
FILT = 128
TOK_DEV = 1024
TOKENS = 16384
GROUPS = 512
N_SEQ = 16


def with_spikes(drawn, rng, source, target, parts, factor):
    def block_of(dim):
        return (jnp.arange(drawn.shape[dim]) // (drawn.shape[dim] // parts)).reshape((-1,) + (1,) * (drawn.ndim - 1 - dim))

    first = jax.random.permutation(rng, parts)[block_of(target)]
    far = (block_of(target) + parts // 2) % parts
    return jnp.where((block_of(source) == first) | (block_of(source) == far), factor * drawn, drawn)


def levels(own_key, dims, cuts, smallest, high):
    factor_of, own = 1.0, jax.random.fold_in(own_key, 6)
    for dim, parts in cuts:
        heights = jnp.exp(jax.random.uniform(jax.random.fold_in(own, dim), (parts,), jnp.float32, smallest / len(cuts), high / len(cuts)))
        factor_of = factor_of * jnp.repeat(heights, dims[dim] // parts).reshape([-1 if axis == dim else 1 for axis in range(len(dims))])
    return factor_of


def bell_draw(own_key, dims, scale, most, pieces=(), kind=jnp.bfloat16):
    result = scale * jax.random.normal(own_key, dims, jnp.float32)
    if pieces:
        result = result * levels(own_key, dims, pieces, -0.22, 0.18)
    return jnp.clip(result, -most, most).astype(kind)


def noise_with(stream_key, extent, scale, limit, split, heavy, kind=jnp.bfloat16):
    entries = scale * jax.random.normal(stream_key, extent, jnp.float32)
    if split:
        entries = entries * levels(stream_key, extent, split, -0.22, 0.18)
    return jnp.clip(with_spikes(entries, jax.random.fold_in(stream_key, 3), *heavy), -limit, limit).astype(kind)


def setup_inputs(seed: int = 0) -> dict:
    seeds = jax.random.split(jax.random.key(seed), 7)
    queries = bell_draw(seeds[0], (TOKENS, D), 1.0, 6.0, ((0, 16), (1, 8)))
    keys = bell_draw(seeds[1], (TOKENS, D), 1.0, 6.0, ((0, 16), (1, 8)))
    values = bell_draw(seeds[2], (TOKENS, D), 1.0, 6.0, ((0, 16), (1, 8)))
    filters = bell_draw(seeds[3], (GROUPS, FILT), FILT ** -0.5, 0.5, ((0, 8),))
    grad_out = noise_with(seeds[4], (TOKENS, FEAT_OUT), 1.0, 6.0, ((0, 16), (1, 8)), (0, 1, 16, 2.0))
    out_weight = bell_draw(seeds[5], (FEAT_OUT, D), FEAT_OUT ** -0.5, 0.09375, ((0, 16), (1, 8)))
    return {"queries": queries, "keys": keys, "values": values, "filters": filters, "grad_out": grad_out, "out_weight": out_weight}


def lag_tables(filter_taps):
    inner = jnp.arange(FILT, dtype=jnp.int32)[:, None]
    outer = jnp.arange(2 * FILT, dtype=jnp.int32)[None, :]
    back_lag = inner + FILT - outer
    ahead_lag = outer - inner
    back_ok = (back_lag >= 0) & (back_lag < FILT)
    ahead_ok = (ahead_lag >= 0) & (ahead_lag < FILT)
    back = jnp.where(back_ok[None], filter_taps[:, jnp.clip(back_lag, 0, FILT - 1)], 0.0)
    ahead = jnp.where(ahead_ok[None], filter_taps[:, jnp.clip(ahead_lag, 0, FILT - 1)], 0.0)
    return back, ahead


def paired(extended, groups):
    blocks = extended.reshape(-1, FILT, groups, GROUP)
    return jnp.concatenate([blocks[:-1], blocks[1:]], axis=1)


def lag_sums(lag_matrix):
    groups, inner, outer = lag_matrix.shape
    flat = lag_matrix.reshape(groups, inner * outer)
    flat = jnp.pad(flat, ((0, 0), (0, inner)))
    skewed = flat.reshape(groups, inner, outer + 1)
    return jnp.sum(skewed[:, :, 1:inner + 1], axis=1)[:, ::-1]


def reference(queries, keys, values, filters, grad_out, out_weight):
    single = jnp.float32
    total_rows, width = queries.shape
    out_width = grad_out.shape[1]
    groups = width // GROUP
    nblocks = total_rows // FILT
    product = (keys.astype(single) * values.astype(single)).astype(jnp.bfloat16)
    extended = jnp.concatenate([jnp.zeros((FILT, width), jnp.bfloat16), product], axis=0)
    pairs = paired(extended, groups).astype(single)
    back, ahead = lag_tables(filters.astype(single))
    mixed = jnp.einsum('gim,bmgs->bigs', back, pairs).reshape(total_rows, width)
    gated = (queries.astype(single) * mixed).astype(jnp.bfloat16)
    grad_gated = jnp.dot(grad_out, out_weight, preferred_element_type=single).astype(jnp.bfloat16)
    grad_queries = (grad_gated.astype(single) * mixed).astype(jnp.bfloat16)
    grad_mixed = (grad_gated.astype(single) * queries.astype(single)).astype(jnp.bfloat16)
    grad_ext = jnp.concatenate([grad_mixed, jnp.zeros((FILT, width), jnp.bfloat16)], axis=0)
    grad_pairs = paired(grad_ext, groups).astype(single)
    grad_product = jnp.einsum('gim,bmgs->bigs', ahead, grad_pairs).reshape(total_rows, width)
    grad_keys = (grad_product * values.astype(single)).astype(jnp.bfloat16)
    grad_values = (grad_product * keys.astype(single)).astype(jnp.bfloat16)
    own_blocks = grad_mixed.astype(single).reshape(nblocks, FILT, groups, GROUP)
    lag_matrix = jnp.einsum('bigs,bmgs->gim', own_blocks, pairs)
    grad_filters = lag_sums(lag_matrix)
    cot_blocks = grad_out.reshape(N_SEQ, TOK_DEV, out_width)
    act_blocks = gated.reshape(N_SEQ, TOK_DEV, width)

    def accumulate(index, carry):
        partial_sum = jnp.dot(cot_blocks[index].T, act_blocks[index], preferred_element_type=single)
        rounded = lax.optimization_barrier(partial_sum.astype(jnp.bfloat16))
        return carry + rounded.astype(single)

    grad_weight = lax.fori_loop(0, N_SEQ, accumulate, jnp.zeros((out_width, width), single))
    return grad_queries, grad_keys, grad_values, grad_filters, grad_weight.astype(jnp.bfloat16)
```

```python
import jax
import jax.numpy as jnp
from jax import lax
from jax.experimental import pallas as pl
from jax.experimental.pallas import tpu as pltpu
from jax.sharding import PartitionSpec as P

F32 = jnp.float32
BF16 = jnp.bfloat16
MESH = pl.DeviceIdType.MESH
FILT = 128
TOK = 1024
CH = 1024
OWN = 256
EB = 512
HALF, QUART = 512, 256

W_COPIES, A_COPIES, R_COPIES = 32, 13, 40
A_BASE = W_COPIES
R_BASE = A_BASE + A_COPIES
H_BASE = R_BASE + R_COPIES
F_BASE = H_BASE + 2
COPIES = F_BASE + 6


def kernel(
    q_hbm, k_hbm, v_hbm, f_ref, a_hbm, w_hbm,
    gq_hbm, gk_hbm, gv_hbm, gf_hbm, gw_hbm,
    kb, vb, qb, pe, ge, mx, gt, afull, wfull, part,
    bq, bf, tbl, rback, rahead, gfr, g1, r1, g2, r2, gfo, gwo,
    ssem, rsem, lsem,
):
    s = lax.axis_index("seq")
    h = lax.axis_index("ch")
    y, z = s // 4, s % 4
    xx, core = h // 2, h % 2

    def at(c, by):
        return (c + by + 4) % 4

    def dev_y(by):
        return (at(y, by) * 4 + z, h)

    def dev_z(by):
        return (y * 4 + at(z, by), h)

    def dev_x(by):
        return (s, at(xx, by) * 2 + core)

    sibling = (s, xx * 2 + (1 - core))
    after = ((s + 1) % 16, h)
    before = ((s + 15) % 16, h)

    sent = []

    def send(src, dst, k, dev):
        c = pltpu.make_async_remote_copy(
            src_ref=src, dst_ref=dst, send_sem=ssem.at[k], recv_sem=rsem.at[k],
            device_id=dev, device_id_type=MESH,
        )
        c.start()
        sent.append(c)

    def arrived(dst, k):
        pltpu.make_async_remote_copy(
            src_ref=dst, dst_ref=dst, send_sem=ssem.at[k], recv_sem=rsem.at[k],
            device_id=sibling, device_id_type=MESH,
        ).wait_recv()

    def local(src, dst, k):
        c = pltpu.make_async_copy(src, dst, lsem.at[k])
        c.start()
        return c

    ld_k = local(k_hbm, kb, 0)
    ld_v = local(v_hbm, vb, 1)
    ld_w = local(w_hbm, wfull.at[pl.ds(pl.multiple_of(s * OWN, OWN), OWN)], 2)
    ld_a = local(a_hbm, afull.at[h], 3)
    ld_q = local(q_hbm, qb, 4)

    peers = [dev_y(1), dev_y(2), dev_y(3), dev_z(1), dev_z(2), dev_z(3), dev_x(1), dev_x(3), sibling, after, before]
    bar = pltpu.get_barrier_semaphore()
    for p in peers:
        pl.semaphore_signal(bar, inc=1, device_id=p, device_id_type=MESH)
    pl.semaphore_wait(bar, len(peers))

    def wrows(yy, zz, start, size):
        return wfull.at[pl.ds(pl.multiple_of((yy * 4 + zz) * OWN + start, 64), size)]

    own_w = wfull.at[pl.ds(pl.multiple_of(s * OWN, OWN), OWN)]
    for k, dev in ((0, dev_z(1)), (1, dev_z(-1)), (2, dev_y(1)), (3, dev_y(-1))):
        send(w_hbm, own_w, k, dev)

    def ablk(bx, bc, half=None):
        r = afull.at[at(xx, bx) * 2 + bc]
        return r if half is None else r.at[pl.ds(half * 512, 512)]

    own_lo, own_hi = ablk(0, core, 0), ablk(0, core, 1)
    send(a_hbm.at[pl.ds(0, 512)], own_lo, A_BASE + 0, dev_x(1))
    send(a_hbm.at[pl.ds(512, 512)], own_hi, A_BASE + 1, dev_x(-1))
    send(a_hbm.at[pl.ds(512, 512)], own_hi, A_BASE + 2, dev_x(1))
    send(a_hbm.at[pl.ds(0, 512)], own_lo, A_BASE + 3, dev_x(-1))
    send(a_hbm, ablk(0, core), A_BASE + 4, sibling)

    def w1_z_minus():
        arrived(wrows(y, at(z, -1), 0, 256), 0)
        r = wrows(y, at(z, -1), 0, 128)
        send(r, r, 4, dev_z(1))
        send(r, r, 8, dev_y(1))
        send(r, r, 9, dev_y(-1))

    def w1_z_plus():
        arrived(wrows(y, at(z, 1), 0, 256), 1)
        r = wrows(y, at(z, 1), 128, 128)
        send(r, r, 5, dev_z(-1))
        r = wrows(y, at(z, 1), 0, 128)
        send(r, r, 10, dev_y(1))
        send(r, r, 11, dev_y(-1))

    def w1_y_minus():
        arrived(wrows(at(y, -1), z, 0, 256), 2)
        r = wrows(at(y, -1), z, 0, 128)
        send(r, r, 6, dev_y(1))
        r = wrows(at(y, -1), z, 128, 128)
        send(r, r, 14, dev_z(1))
        send(r, r, 15, dev_z(-1))

    def w1_y_plus():
        arrived(wrows(at(y, 1), z, 0, 256), 3)
        r = wrows(at(y, 1), z, 128, 128)
        send(r, r, 7, dev_y(-1))
        send(r, r, 16, dev_z(1))
        send(r, r, 17, dev_z(-1))

    def w2():
        r = wrows(y, at(z, 2), 0, 128)
        arrived(r, 4)
        send(r, r, 12, dev_y(1))
        send(r, r, 13, dev_y(-1))
        r = wrows(at(y, 2), z, 128, 128)
        arrived(r, 7)
        send(r, r, 18, dev_z(1))
        send(r, r, 19, dev_z(-1))

    def w3(i):
        bz = (-1, 1, 2)[i]
        r = wrows(at(y, -1), at(z, bz), 0, 128)
        arrived(r, 8 + 2 * i)
        r = wrows(at(y, -1), at(z, bz), 0, 64)
        send(r, r, 20 + 2 * i, dev_y(1))
        r = wrows(at(y, 1), at(z, bz), 0, 128)
        arrived(r, 9 + 2 * i)
        r = wrows(at(y, 1), at(z, bz), 64, 64)
        send(r, r, 21 + 2 * i, dev_y(-1))
        r = wrows(at(y, bz), at(z, -1), 128, 128)
        arrived(r, 14 + 2 * i)
        r = wrows(at(y, bz), at(z, -1), 128, 64)
        send(r, r, 26 + 2 * i, dev_z(1))
        r = wrows(at(y, bz), at(z, 1), 128, 128)
        arrived(r, 15 + 2 * i)
        r = wrows(at(y, bz), at(z, 1), 192, 64)
        send(r, r, 27 + 2 * i, dev_z(-1))

    def w_last():
        arrived(wrows(y, at(z, 2), 128, 128), 5)
        arrived(wrows(at(y, 2), z, 0, 128), 6)
        for i in range(3):
            bz = (-1, 1, 2)[i]
            arrived(wrows(at(y, 2), at(z, bz), 0, 64), 20 + 2 * i)
            arrived(wrows(at(y, 2), at(z, bz), 64, 64), 21 + 2 * i)
            arrived(wrows(at(y, bz), at(z, 2), 128, 64), 26 + 2 * i)
            arrived(wrows(at(y, bz), at(z, 2), 192, 64), 27 + 2 * i)

    def a1():
        r = ablk(-1, core, 0)
        arrived(r, A_BASE + 0)
        send(r, r, A_BASE + 5, dev_x(1))
        send(r, r, A_BASE + 7, sibling)
        r = ablk(1, core, 1)
        arrived(r, A_BASE + 1)
        send(r, r, A_BASE + 6, dev_x(-1))
        send(r, r, A_BASE + 8, sibling)

    def a2():
        r = ablk(-1, core, 1)
        arrived(r, A_BASE + 2)
        send(r, r, A_BASE + 9, sibling)
        r = ablk(1, core, 0)
        arrived(r, A_BASE + 3)
        send(r, r, A_BASE + 10, sibling)

    def a3():
        r = ablk(2, core, 0)
        arrived(r, A_BASE + 5)
        send(r, r, A_BASE + 11, sibling)
        r = ablk(2, core, 1)
        arrived(r, A_BASE + 6)
        send(r, r, A_BASE + 12, sibling)

    def a_sib_own():
        arrived(ablk(0, 1 - core), A_BASE + 4)

    def a_sib_near():
        arrived(ablk(-1, 1 - core, 0), A_BASE + 7)
        arrived(ablk(-1, 1 - core, 1), A_BASE + 9)
        arrived(ablk(1, 1 - core, 1), A_BASE + 8)
        arrived(ablk(1, 1 - core, 0), A_BASE + 10)

    def a_sib_far():
        arrived(ablk(2, 1 - core, 0), A_BASE + 11)
        arrived(ablk(2, 1 - core, 1), A_BASE + 12)

    def rs_pieces(hf, stage, along_z, other):
        def chunk(by, q=None):
            idx = other * 4 + at(z, by) if along_z else at(y, by) * 4 + other
            if q is None:
                return part.at[idx, pl.ds(hf * HALF, HALF)]
            return part.at[idx, pl.ds(hf * HALF + q * QUART, QUART)]

        return chunk

    def rs(hf, stage, i):
        along_z = (hf == 0) == (stage == 0)
        other = at(y if along_z else z, i)
        dev = dev_z if along_z else dev_y
        chunk = rs_pieces(hf, stage, along_z, other)
        slot = hf * 5 + (i if stage == 0 else 4)
        base = R_BASE + slot * 4
        half_in = bq.at[slot]
        full_in = bf.at[slot]

        def start():
            send(chunk(2, 0), half_in.at[0], base + 0, dev(-1))
            send(chunk(2, 1), half_in.at[1], base + 1, dev(1))

        def mid():
            for q, by in ((0, -1), (1, 1)):
                arrived(half_in.at[q], base + q)
                c = chunk(by, q)
                c[...] = (c[...].astype(F32) + half_in[q].astype(F32)).astype(BF16)
                send(chunk(by), full_in.at[q], base + 2 + q, dev(by))

        def fin():
            arrived(full_in.at[0], base + 2)
            arrived(full_in.at[1], base + 3)
            c = chunk(0)
            total = c[...].astype(F32) + full_in[0].astype(F32) + full_in[1].astype(F32)
            if stage == 0:
                c[...] = total.astype(BF16)
            else:
                gwo[:, hf * HALF : (hf + 1) * HALF] = total.astype(BF16).T

        return start, mid, fin

    ld_k.wait()
    ld_v.wait()

    def product_rows(r):
        rows = pl.ds(r, 128)
        pe[pl.ds(r + FILT, 128)] = (kb[rows].astype(F32) * vb[rows].astype(F32)).astype(BF16)

    product_rows(TOK - FILT)
    send(pe.at[pl.ds(TOK, FILT)], pe.at[pl.ds(0, FILT)], H_BASE, after)

    def product_loop(i, _):
        product_rows(pl.multiple_of(i * 128, 128))
        return 0

    lax.fori_loop(0, TOK // 128 - 1, product_loop, 0)

    tap = lax.broadcasted_iota(jnp.int32, (FILT, 256), 0)
    lane = lax.broadcasted_iota(jnp.int32, (FILT, 256), 1)
    f = f_ref[...]
    rback[...] = jnp.dot(f, (lane == FILT - tap).astype(F32).astype(BF16), preferred_element_type=F32)
    rahead[...] = jnp.dot(f, (lane == tap).astype(F32).astype(BF16), preferred_element_type=F32)
    group_of = (lane % 128) // 16

    def lanes_of(L):
        return pl.ds(pl.multiple_of(L * 128, 128), 128)

    def make_table(rows_ref, L):
        rows = rows_ref[pl.ds(pl.multiple_of(L * 8, 8), 8), :]
        for g in range(8):
            wide = jnp.broadcast_to(rows[g : g + 1, :], (FILT, 256))
            tbl[g * FILT : (g + 1) * FILT, :] = pltpu.roll(wide, 0, 1, stride=1, stride_axis=0).astype(BF16)

    def windows(ref, p, lanes):
        return jnp.concatenate([ref[pl.ds(p * 256, 256), lanes], ref[pl.ds(p * 256 + 128, 256), lanes]], axis=1)

    def filtered(ref, p, lanes):
        res = jnp.dot(tbl[...], windows(ref, p, lanes), preferred_element_type=F32)
        out = res[0:FILT]
        for g in range(1, 8):
            out = jnp.where(group_of == g, res[g * FILT : (g + 1) * FILT], out)
        return jnp.concatenate([out[:, :128], out[:, 128:]], axis=0)

    def conv_mixed(L, _):
        lanes = lanes_of(L)
        make_table(rback, L)
        for p in range(4):
            m = filtered(pe, p, lanes)
            rows = pl.ds(p * 256, 256)
            mx[rows, lanes] = m.astype(BF16)
            gated = (qb[rows, lanes].astype(F32) * m).astype(BF16)
            gt[lanes, rows] = gated.T
        return 0

    arrived(pe.at[pl.ds(0, FILT)], H_BASE)

    @pl.when(s == 0)
    def _():
        pe[pl.ds(0, FILT)] = jnp.zeros((FILT, CH), BF16)

    ld_q.wait()
    lax.fori_loop(0, 4, conv_mixed, 0)
    w1_z_minus()
    w1_z_plus()
    w1_y_minus()
    w1_y_plus()
    lax.fori_loop(4, 8, conv_mixed, 0)
    ld_w.wait()
    ld_a.wait()
    a1()

    def weight_grad(bx, bc):
        blk = at(xx, bx) * 2 + bc

        def one(u, _):
            cols = pl.ds(pl.multiple_of(u * 256, 256), 256)
            r = jnp.dot(gt[...], afull[blk, :, cols], preferred_element_type=F32)
            part[blk * 2 + u] = r.astype(BF16)
            return 0

        lax.fori_loop(0, 2, one, 0)

    a_sib_own()
    weight_grad(0, 0)
    w2()
    weight_grad(0, 1)
    a2()
    w3(0)
    w3(1)
    weight_grad(-1, core)
    weight_grad(1, core)
    a3()
    w3(2)
    a_sib_near()
    weight_grad(-1, 1 - core)
    weight_grad(1, 1 - core)
    a_sib_far()
    weight_grad(2, 0)
    weight_grad(2, 1)

    first = [rs(hf, 0, i) for i in (2, 1, 3, 0) for hf in (0, 1)]
    second = [rs(hf, 1, 0) for hf in (0, 1)]
    for start, _, _ in first:
        start()
    w_last()

    def gated_grad(n, _):
        cols = pl.ds(pl.multiple_of(n * 256, 256), 256)
        acc = jnp.dot(afull[0], wfull[pl.ds(0, EB), cols], preferred_element_type=F32)
        for b in range(1, 8):
            acc = acc + jnp.dot(afull[b], wfull[pl.ds(b * EB, EB), cols], preferred_element_type=F32)
        gg = acc.astype(BF16).astype(F32)
        ge[pl.ds(0, TOK), cols] = (gg * qb[:, cols].astype(F32)).astype(BF16)
        mx[:, cols] = (gg * mx[:, cols].astype(F32)).astype(BF16)
        return 0

    lax.fori_loop(0, 2, gated_grad, 0)
    for _, mid, _ in first[:4]:
        mid()
    lax.fori_loop(2, 4, gated_grad, 0)
    send(ge.at[pl.ds(0, FILT)], ge.at[pl.ds(TOK, FILT)], H_BASE + 1, before)
    st_q = local(mx, gq_hbm, 4)
    for _, mid, _ in first[4:]:
        mid()

    flip = (lax.broadcasted_iota(jnp.int32, (FILT, FILT), 0) + lax.broadcasted_iota(jnp.int32, (FILT, FILT), 1) == FILT - 1)
    flip = flip.astype(F32).astype(BF16)

    def lag_products(L, _):
        lanes = lanes_of(L)
        acc = None
        for p in range(4):
            own = jnp.concatenate([ge[pl.ds(p * 256, 128), lanes], ge[pl.ds(p * 256 + 128, 128), lanes]], axis=1)
            own = jnp.dot(flip, own, preferred_element_type=F32)
            lhs = jnp.concatenate([jnp.where(group_of == g, own, 0.0).astype(BF16) for g in range(8)], axis=0)
            d = lax.dot_general(lhs, windows(pe, p, lanes), (((1,), (1,)), ((), ())), preferred_element_type=F32)
            acc = d if acc is None else acc + d
        sums = []
        for g in range(8):
            skew = pltpu.roll(acc[g * FILT : (g + 1) * FILT], 0, 1, stride=1, stride_axis=0)
            sums.append(jnp.sum(skew, axis=0, keepdims=True))
        gfr[pl.ds(pl.multiple_of(L * 8, 8), 8), :] = jnp.concatenate(sums, axis=0)
        return 0

    gfr[...] = jnp.zeros((128, 256), F32)
    lax.fori_loop(0, 8, lag_products, 0)
    pick = (lane == 255 - tap).astype(F32).astype(BF16)
    hi = gfr[...].astype(BF16)
    lo = (gfr[...] - hi.astype(F32)).astype(BF16)
    nt = (((1,), (1,)), ((), ()))
    taps = lax.dot_general(pick, hi, nt, preferred_element_type=F32) + lax.dot_general(pick, lo, nt, preferred_element_type=F32)
    for t in range(16):
        g1[t % 4, t // 4] = taps[t * 8 : (t + 1) * 8]
    for d in (1, 2, 3):
        send(g1.at[at(z, d)], r1.at[d - 1], F_BASE + d - 1, dev_z(d))
    for _, _, fin in first[:4]:
        fin()

    arrived(ge.at[pl.ds(TOK, FILT)], H_BASE + 1)

    @pl.when(s == 15)
    def _():
        ge[pl.ds(TOK, FILT)] = jnp.zeros((FILT, CH), BF16)

    def conv_grad(L, _):
        lanes = lanes_of(L)
        make_table(rahead, L)
        for p in range(4):
            m = filtered(ge, p, lanes)
            rows = pl.ds(p * 256, 256)
            keys, values = kb[rows, lanes].astype(F32), vb[rows, lanes].astype(F32)
            kb[rows, lanes] = (m * values).astype(BF16)
            vb[rows, lanes] = (m * keys).astype(BF16)
        return 0

    lax.fori_loop(0, 4, conv_grad, 0)
    for _, _, fin in first[4:]:
        fin()
    for start, _, _ in second:
        start()
    for d in (1, 2, 3):
        arrived(r1.at[d - 1], F_BASE + d - 1)
    g2[...] = g1[z] + r1[0] + r1[1] + r1[2]
    for d in (1, 2, 3):
        send(g2.at[at(y, d)], r2.at[d - 1], F_BASE + 2 + d, dev_y(d))
    lax.fori_loop(4, 8, conv_grad, 0)
    st_k = local(kb, gk_hbm, 0)
    st_v = local(vb, gv_hbm, 1)
    for _, mid, _ in second:
        mid()
    for d in (1, 2, 3):
        arrived(r2.at[d - 1], F_BASE + 2 + d)
    total = g2[y] + r2[0] + r2[1] + r2[2]
    gfo[...] = total.T[:64]
    st_f = local(gfo, gf_hbm, 2)
    for _, _, fin in second:
        fin()
    st_w = local(gwo, gw_hbm, 3)
    for c in sent:
        c.wait_send()
    for c in (st_q, st_k, st_v, st_f, st_w):
        c.wait()


def shards(queries, keys, values, filters, grad_out, out_weight):
    hbm = pl.BlockSpec(memory_space=pl.ANY)
    vm = pltpu.VMEM
    out = pl.pallas_call(
        kernel,
        out_shape=(
            jax.ShapeDtypeStruct((TOK, CH), BF16),
            jax.ShapeDtypeStruct((TOK, CH), BF16),
            jax.ShapeDtypeStruct((TOK, CH), BF16),
            jax.ShapeDtypeStruct((64, 8), F32),
            jax.ShapeDtypeStruct((OWN, CH), BF16),
        ),
        in_specs=[hbm, hbm, hbm, pl.BlockSpec(memory_space=pltpu.VMEM), hbm, hbm],
        out_specs=(hbm,) * 5,
        scratch_shapes=[
            vm((TOK, CH), BF16),
            vm((TOK, CH), BF16),
            vm((TOK, CH), BF16),
            vm((TOK + FILT, CH), BF16),
            vm((TOK + FILT, CH), BF16),
            vm((TOK, CH), BF16),
            vm((CH, TOK), BF16),
            vm((8, TOK, EB), BF16),
            vm((4096, CH), BF16),
            vm((16, CH, OWN), BF16),
            vm((10, 2, QUART, OWN), BF16),
            vm((10, 2, HALF, OWN), BF16),
            vm((1024, 256), BF16),
            vm((64, 256), F32),
            vm((64, 256), F32),
            vm((128, 256), F32),
            vm((4, 4, 8, 128), F32),
            vm((3, 4, 8, 128), F32),
            vm((4, 8, 128), F32),
            vm((3, 8, 128), F32),
            vm((64, 8), F32),
            vm((OWN, CH), BF16),
            pltpu.SemaphoreType.DMA((COPIES,)),
            pltpu.SemaphoreType.DMA((COPIES,)),
            pltpu.SemaphoreType.DMA((5,)),
        ],
        compiler_params=pltpu.CompilerParams(
            collective_id=0, has_side_effects=True, vmem_limit_bytes=63 * 1024 * 1024
        ),
        name="hyena_bwd",
    )(queries, keys, values, filters, grad_out, out_weight)
    return out


def solution(mesh):
    return jax.shard_map(
        shards,
        mesh=mesh,
        in_specs=(
            P("seq", "ch"),
            P("seq", "ch"),
            P("seq", "ch"),
            P("ch", None),
            P("seq", "ch"),
            P("seq", "ch"),
        ),
        out_specs=(P("seq", "ch"), P("seq", "ch"), P("seq", "ch"), P("ch", "seq"), P("seq", "ch")),
        check_vma=False,
    )
```

```python
import jax
import jax.numpy as jnp
from jax import lax
from jax.experimental import pallas as pl
from jax.experimental.pallas import tpu as pltpu
from jax.sharding import PartitionSpec as P

F32 = jnp.float32
BF16 = jnp.bfloat16
MESH = pl.DeviceIdType.MESH
FILT = 128
TOK = 1024
CH = 1024
OWN = 256
EB = 512
HALF, QUART = 512, 256

W_COPIES, A_COPIES, R_COPIES = 32, 13, 40
A_BASE = W_COPIES
R_BASE = A_BASE + A_COPIES
H_BASE = R_BASE + R_COPIES
F_BASE = H_BASE + 2
COPIES = F_BASE + 6


def kernel(
    q_hbm, k_hbm, v_hbm, f_ref, a_hbm, w_hbm,
    mx, kb, vb, gfo, gwo,
    qb, pe, ge, gt, afull, wfull, part,
    bq, bf, tbl, rback, rahead, gfr, g1, r1, g2, r2,
    ssem, rsem, lsem,
):
    s = lax.axis_index("seq")
    h = lax.axis_index("ch")
    y, z = s // 4, s % 4
    xx, core = h // 2, h % 2

    def at(c, by):
        return (c + by + 4) % 4

    def dev_y(by):
        return (at(y, by) * 4 + z, h)

    def dev_z(by):
        return (y * 4 + at(z, by), h)

    def dev_x(by):
        return (s, at(xx, by) * 2 + core)

    sibling = (s, xx * 2 + (1 - core))
    after = ((s + 1) % 16, h)
    before = ((s + 15) % 16, h)

    sent = []

    def send(src, dst, k, dev):
        c = pltpu.make_async_remote_copy(
            src_ref=src, dst_ref=dst, send_sem=ssem.at[k], recv_sem=rsem.at[k],
            device_id=dev, device_id_type=MESH,
        )
        c.start()
        sent.append(c)

    def arrived(dst, k):
        pltpu.make_async_remote_copy(
            src_ref=dst, dst_ref=dst, send_sem=ssem.at[k], recv_sem=rsem.at[k],
            device_id=sibling, device_id_type=MESH,
        ).wait_recv()

    def local(src, dst, k):
        c = pltpu.make_async_copy(src, dst, lsem.at[k])
        c.start()
        return c

    own_w = wfull.at[pl.ds(pl.multiple_of(s * OWN, OWN), OWN)]
    tail, rest = pl.ds(TOK - FILT, FILT), pl.ds(0, TOK - FILT)
    ld_tail = [local(k_hbm.at[tail], kb.at[tail], 0), local(v_hbm.at[tail], vb.at[tail], 1)]
    ld_rest = [local(k_hbm.at[rest], kb.at[rest], 2), local(v_hbm.at[rest], vb.at[rest], 3)]
    ld_q = local(q_hbm, qb, 4)
    ld_w = local(w_hbm, own_w, 5)
    ld_a = local(a_hbm, afull.at[h], 6)

    peers = [dev_y(1), dev_y(2), dev_y(3), dev_z(1), dev_z(2), dev_z(3), dev_x(1), dev_x(3), sibling, after, before]
    bar = pltpu.get_barrier_semaphore()
    for p in peers:
        pl.semaphore_signal(bar, inc=1, device_id=p, device_id_type=MESH)

    def product_rows(r):
        rows = pl.ds(r, 128)
        pe[pl.ds(r + FILT, 128)] = (kb[rows].astype(F32) * vb[rows].astype(F32)).astype(BF16)

    for c in ld_tail:
        c.wait()
    product_rows(TOK - FILT)
    pl.semaphore_wait(bar, len(peers))
    send(pe.at[pl.ds(TOK, FILT)], pe.at[pl.ds(0, FILT)], H_BASE, after)

    def wrows(yy, zz, start, size):
        return wfull.at[pl.ds(pl.multiple_of((yy * 4 + zz) * OWN + start, 64), size)]

    for k, dev in ((0, dev_z(1)), (1, dev_z(-1)), (2, dev_y(1)), (3, dev_y(-1))):
        send(w_hbm, own_w, k, dev)

    def ablk(bx, bc, half=None):
        r = afull.at[at(xx, bx) * 2 + bc]
        return r if half is None else r.at[pl.ds(half * 512, 512)]

    own_lo, own_hi = ablk(0, core, 0), ablk(0, core, 1)
    send(a_hbm.at[pl.ds(0, 512)], own_lo, A_BASE + 0, dev_x(1))
    send(a_hbm.at[pl.ds(512, 512)], own_hi, A_BASE + 1, dev_x(-1))
    send(a_hbm.at[pl.ds(512, 512)], own_hi, A_BASE + 2, dev_x(1))
    send(a_hbm.at[pl.ds(0, 512)], own_lo, A_BASE + 3, dev_x(-1))
    send(a_hbm, ablk(0, core), A_BASE + 4, sibling)

    def w1_z_minus():
        arrived(wrows(y, at(z, -1), 0, 256), 0)
        r = wrows(y, at(z, -1), 0, 128)
        send(r, r, 4, dev_z(1))
        send(r, r, 8, dev_y(1))
        send(r, r, 9, dev_y(-1))

    def w1_z_plus():
        arrived(wrows(y, at(z, 1), 0, 256), 1)
        r = wrows(y, at(z, 1), 128, 128)
        send(r, r, 5, dev_z(-1))
        r = wrows(y, at(z, 1), 0, 128)
        send(r, r, 10, dev_y(1))
        send(r, r, 11, dev_y(-1))

    def w1_y_minus():
        arrived(wrows(at(y, -1), z, 0, 256), 2)
        r = wrows(at(y, -1), z, 0, 128)
        send(r, r, 6, dev_y(1))
        r = wrows(at(y, -1), z, 128, 128)
        send(r, r, 14, dev_z(1))
        send(r, r, 15, dev_z(-1))

    def w1_y_plus():
        arrived(wrows(at(y, 1), z, 0, 256), 3)
        r = wrows(at(y, 1), z, 128, 128)
        send(r, r, 7, dev_y(-1))
        send(r, r, 16, dev_z(1))
        send(r, r, 17, dev_z(-1))

    def w2():
        r = wrows(y, at(z, 2), 0, 128)
        arrived(r, 4)
        send(r, r, 12, dev_y(1))
        send(r, r, 13, dev_y(-1))
        r = wrows(at(y, 2), z, 128, 128)
        arrived(r, 7)
        send(r, r, 18, dev_z(1))
        send(r, r, 19, dev_z(-1))

    def w3(i):
        bz = (-1, 1, 2)[i]
        r = wrows(at(y, -1), at(z, bz), 0, 128)
        arrived(r, 8 + 2 * i)
        r = wrows(at(y, -1), at(z, bz), 0, 64)
        send(r, r, 20 + 2 * i, dev_y(1))
        r = wrows(at(y, 1), at(z, bz), 0, 128)
        arrived(r, 9 + 2 * i)
        r = wrows(at(y, 1), at(z, bz), 64, 64)
        send(r, r, 21 + 2 * i, dev_y(-1))
        r = wrows(at(y, bz), at(z, -1), 128, 128)
        arrived(r, 14 + 2 * i)
        r = wrows(at(y, bz), at(z, -1), 128, 64)
        send(r, r, 26 + 2 * i, dev_z(1))
        r = wrows(at(y, bz), at(z, 1), 128, 128)
        arrived(r, 15 + 2 * i)
        r = wrows(at(y, bz), at(z, 1), 192, 64)
        send(r, r, 27 + 2 * i, dev_z(-1))

    def w_last():
        arrived(wrows(y, at(z, 2), 128, 128), 5)
        arrived(wrows(at(y, 2), z, 0, 128), 6)
        for i in range(3):
            bz = (-1, 1, 2)[i]
            arrived(wrows(at(y, 2), at(z, bz), 0, 64), 20 + 2 * i)
            arrived(wrows(at(y, 2), at(z, bz), 64, 64), 21 + 2 * i)
            arrived(wrows(at(y, bz), at(z, 2), 128, 64), 26 + 2 * i)
            arrived(wrows(at(y, bz), at(z, 2), 192, 64), 27 + 2 * i)

    def a1():
        r = ablk(-1, core, 0)
        arrived(r, A_BASE + 0)
        send(r, r, A_BASE + 5, dev_x(1))
        send(r, r, A_BASE + 7, sibling)
        r = ablk(1, core, 1)
        arrived(r, A_BASE + 1)
        send(r, r, A_BASE + 6, dev_x(-1))
        send(r, r, A_BASE + 8, sibling)

    def a2():
        r = ablk(-1, core, 1)
        arrived(r, A_BASE + 2)
        send(r, r, A_BASE + 9, sibling)
        r = ablk(1, core, 0)
        arrived(r, A_BASE + 3)
        send(r, r, A_BASE + 10, sibling)

    def a3():
        r = ablk(2, core, 0)
        arrived(r, A_BASE + 5)
        send(r, r, A_BASE + 11, sibling)
        r = ablk(2, core, 1)
        arrived(r, A_BASE + 6)
        send(r, r, A_BASE + 12, sibling)

    def a_sib_own():
        arrived(ablk(0, 1 - core), A_BASE + 4)

    def a_sib_near():
        arrived(ablk(-1, 1 - core, 0), A_BASE + 7)
        arrived(ablk(-1, 1 - core, 1), A_BASE + 9)
        arrived(ablk(1, 1 - core, 1), A_BASE + 8)
        arrived(ablk(1, 1 - core, 0), A_BASE + 10)

    def a_sib_far():
        arrived(ablk(2, 1 - core, 0), A_BASE + 11)
        arrived(ablk(2, 1 - core, 1), A_BASE + 12)

    def rs_pieces(hf, stage, along_z, other):
        def chunk(by, q=None):
            idx = other * 4 + at(z, by) if along_z else at(y, by) * 4 + other
            if q is None:
                return part.at[idx, pl.ds(hf * HALF, HALF)]
            return part.at[idx, pl.ds(hf * HALF + q * QUART, QUART)]

        return chunk

    def rs(hf, stage, i):
        along_z = (hf == 0) == (stage == 0)
        other = at(y if along_z else z, i)
        dev = dev_z if along_z else dev_y
        chunk = rs_pieces(hf, stage, along_z, other)
        slot = hf * 5 + (i if stage == 0 else 4)
        base = R_BASE + slot * 4
        half_in = bq.at[slot]
        full_in = bf.at[slot]

        def start():
            send(chunk(2, 0), half_in.at[0], base + 0, dev(-1))
            send(chunk(2, 1), half_in.at[1], base + 1, dev(1))

        def mid():
            for q, by in ((0, -1), (1, 1)):
                arrived(half_in.at[q], base + q)
                c = chunk(by, q)
                c[...] = (c[...].astype(F32) + half_in[q].astype(F32)).astype(BF16)
                send(chunk(by), full_in.at[q], base + 2 + q, dev(by))

        def fin():
            arrived(full_in.at[0], base + 2)
            arrived(full_in.at[1], base + 3)
            c = chunk(0)
            total = c[...].astype(F32) + full_in[0].astype(F32) + full_in[1].astype(F32)
            if stage == 0:
                c[...] = total.astype(BF16)
            else:
                gwo[hf * HALF : (hf + 1) * HALF] = total.astype(BF16)

        return start, mid, fin

    for c in ld_rest:
        c.wait()

    def product_loop(i, _):
        product_rows(pl.multiple_of(i * 128, 128))
        return 0

    lax.fori_loop(0, TOK // 128 - 1, product_loop, 0)

    tap = lax.broadcasted_iota(jnp.int32, (FILT, 256), 0)
    lane = lax.broadcasted_iota(jnp.int32, (FILT, 256), 1)
    f = f_ref[...]
    rback[...] = jnp.dot(f, (lane == FILT - tap).astype(F32).astype(BF16), preferred_element_type=F32)
    rahead[...] = jnp.dot(f, (lane == tap).astype(F32).astype(BF16), preferred_element_type=F32)
    group_of = (lane % 128) // 16

    def lanes_of(L):
        return pl.ds(pl.multiple_of(L * 128, 128), 128)

    def make_table(rows_ref, L):
        rows = rows_ref[pl.ds(pl.multiple_of(L * 8, 8), 8), :]
        for g in range(8):
            wide = jnp.broadcast_to(rows[g : g + 1, :], (FILT, 256))
            tbl[g * FILT : (g + 1) * FILT, :] = pltpu.roll(wide, 0, 1, stride=1, stride_axis=0).astype(BF16)

    def windows(ref, p, lanes):
        return jnp.concatenate([ref[pl.ds(p * 256, 256), lanes], ref[pl.ds(p * 256 + 128, 256), lanes]], axis=1)

    def filtered(ref, p, lanes):
        res = jnp.dot(tbl[...], windows(ref, p, lanes), preferred_element_type=F32)
        out = res[0:FILT]
        for g in range(1, 8):
            out = jnp.where(group_of == g, res[g * FILT : (g + 1) * FILT], out)
        return jnp.concatenate([out[:, :128], out[:, 128:]], axis=0)

    def conv_mixed(L, _):
        lanes = lanes_of(L)
        make_table(rback, L)
        for p in range(4):
            m = filtered(pe, p, lanes)
            rows = pl.ds(p * 256, 256)
            mx[rows, lanes] = m.astype(BF16)
            gated = (qb[rows, lanes].astype(F32) * m).astype(BF16)
            gt[lanes, rows] = gated.T
        return 0

    arrived(pe.at[pl.ds(0, FILT)], H_BASE)

    @pl.when(s == 0)
    def _():
        pe[pl.ds(0, FILT)] = jnp.zeros((FILT, CH), BF16)

    ld_q.wait()
    lax.fori_loop(0, 8, conv_mixed, 0)
    w1_z_plus()
    w1_y_minus()
    w1_y_plus()
    a1()
    w1_z_minus()
    ld_w.wait()
    ld_a.wait()

    def weight_grad(bx, bc):
        blk = at(xx, bx) * 2 + bc

        def one(u, _):
            cols = pl.ds(pl.multiple_of(u * 256, 256), 256)
            r = jnp.dot(gt[...], afull[blk, :, cols], preferred_element_type=F32)
            part[blk * 2 + u] = r.astype(BF16)
            return 0

        lax.fori_loop(0, 2, one, 0)

    def start_z(bx):
        rs(0, 0, (xx + bx - y + 8) % 4)[0]()

    a_sib_own()
    weight_grad(0, 0)
    weight_grad(0, 1)
    start_z(0)
    w2()
    a2()
    weight_grad(-1, core)
    weight_grad(1, core)
    w3(0)
    a_sib_near()
    weight_grad(-1, 1 - core)
    weight_grad(1, 1 - core)
    start_z(-1)
    start_z(1)
    w3(1)
    a3()
    weight_grad(2, core)
    w3(2)
    a_sib_far()
    weight_grad(2, 1 - core)
    start_z(2)

    order = (2, 1, 3, 0)
    half0 = [rs(0, 0, i) for i in order]
    half1 = [rs(1, 0, i) for i in order]
    end0, end1 = rs(0, 1, 0), rs(1, 1, 0)
    for start, _, _ in half1:
        start()
    w_last()

    def gated_grad(n, _):
        cols = pl.ds(pl.multiple_of(n * 256, 256), 256)
        acc = jnp.dot(afull[0], wfull[pl.ds(0, EB), cols], preferred_element_type=F32)
        for b in range(1, 8):
            acc = acc + jnp.dot(afull[b], wfull[pl.ds(b * EB, EB), cols], preferred_element_type=F32)
        gg = acc.astype(BF16).astype(F32)
        ge[pl.ds(0, TOK), cols] = (gg * qb[:, cols].astype(F32)).astype(BF16)
        mx[:, cols] = (gg * mx[:, cols].astype(F32)).astype(BF16)
        return 0

    for n in range(4):
        lax.fori_loop(n, n + 1, gated_grad, 0)
        half0[n][1]()
    send(ge.at[pl.ds(0, FILT)], ge.at[pl.ds(TOK, FILT)], H_BASE + 1, before)
    for n in range(4):
        half1[n][1]()

    flip = (lax.broadcasted_iota(jnp.int32, (FILT, FILT), 0) + lax.broadcasted_iota(jnp.int32, (FILT, FILT), 1) == FILT - 1)
    flip = flip.astype(F32).astype(BF16)

    def lag_products(L, _):
        lanes = lanes_of(L)
        acc = None
        for p in range(4):
            own = jnp.concatenate([ge[pl.ds(p * 256, 128), lanes], ge[pl.ds(p * 256 + 128, 128), lanes]], axis=1)
            own = jnp.dot(flip, own, preferred_element_type=F32)
            lhs = jnp.concatenate([jnp.where(group_of == g, own, 0.0).astype(BF16) for g in range(8)], axis=0)
            d = lax.dot_general(lhs, windows(pe, p, lanes), (((1,), (1,)), ((), ())), preferred_element_type=F32)
            acc = d if acc is None else acc + d
        sums = []
        for g in range(8):
            skew = pltpu.roll(acc[g * FILT : (g + 1) * FILT], 0, 1, stride=1, stride_axis=0)
            sums.append(jnp.sum(skew, axis=0, keepdims=True))
        gfr[pl.ds(pl.multiple_of(L * 8, 8), 8), :] = jnp.concatenate(sums, axis=0)
        return 0

    gfr[...] = jnp.zeros((128, 256), F32)
    for n in range(4):
        lax.fori_loop(2 * n, 2 * n + 2, lag_products, 0)
        half0[n][2]()
        if n == 0:
            end0[0]()
    end0[1]()
    pick = (lane == 255 - tap).astype(F32).astype(BF16)
    hi = gfr[...].astype(BF16)
    lo = (gfr[...] - hi.astype(F32)).astype(BF16)
    nt = (((1,), (1,)), ((), ()))
    taps = lax.dot_general(pick, hi, nt, preferred_element_type=F32) + lax.dot_general(pick, lo, nt, preferred_element_type=F32)
    for t in range(16):
        g1[t % 4, t // 4] = taps[t * 8 : (t + 1) * 8]
    for d in (1, 2, 3):
        send(g1.at[at(z, d)], r1.at[d - 1], F_BASE + d - 1, dev_z(d))

    arrived(ge.at[pl.ds(TOK, FILT)], H_BASE + 1)

    @pl.when(s == 15)
    def _():
        ge[pl.ds(TOK, FILT)] = jnp.zeros((FILT, CH), BF16)

    def conv_grad(L, _):
        lanes = lanes_of(L)
        make_table(rahead, L)
        for p in range(4):
            m = filtered(ge, p, lanes)
            rows = pl.ds(p * 256, 256)
            keys, values = kb[rows, lanes].astype(F32), vb[rows, lanes].astype(F32)
            kb[rows, lanes] = (m * values).astype(BF16)
            vb[rows, lanes] = (m * keys).astype(BF16)
        return 0

    for n in range(4):
        lax.fori_loop(n, n + 1, conv_grad, 0)
        half1[n][2]()
        if n == 0:
            end1[0]()
    end1[1]()
    for d in (1, 2, 3):
        arrived(r1.at[d - 1], F_BASE + d - 1)
    g2[...] = g1[z] + r1[0] + r1[1] + r1[2]
    for d in (1, 2, 3):
        send(g2.at[at(y, d)], r2.at[d - 1], F_BASE + 2 + d, dev_y(d))
    lax.fori_loop(4, 8, conv_grad, 0)
    for d in (1, 2, 3):
        arrived(r2.at[d - 1], F_BASE + 2 + d)
    total = g2[y] + r2[0] + r2[1] + r2[2]
    gfo[...] = total
    end0[2]()
    end1[2]()
    for c in sent:
        c.wait_send()


def store(gq, gk, gv, gf, gw, gq_out, gk_out, gv_out, gf_out, gw_out, sem):
    copies = [
        pltpu.make_async_copy(src, dst, sem.at[i])
        for i, (src, dst) in enumerate(((gq, gq_out), (gk, gk_out), (gv, gv_out)))
    ]
    for c in copies:
        c.start()
    gw_out[...] = gw[...].T
    gf_out[...] = gf[:, :64]
    for c in copies:
        c.wait()


def shards(queries, keys, values, filters, grad_out, out_weight):
    hbm = pl.BlockSpec(memory_space=pl.ANY)
    vm = pltpu.VMEM
    out = pl.pallas_call(
        kernel,
        out_shape=(
            vm((TOK, CH), BF16),
            vm((TOK, CH), BF16),
            vm((TOK, CH), BF16),
            vm((8, 128), F32),
            vm((CH, OWN), BF16),
        ),
        in_specs=[hbm, hbm, hbm, pl.BlockSpec(memory_space=pltpu.VMEM), hbm, hbm],
        out_specs=(pl.BlockSpec(memory_space=pltpu.VMEM),) * 5,
        scratch_shapes=[
            vm((TOK, CH), BF16),
            vm((TOK + FILT, CH), BF16),
            vm((TOK + FILT, CH), BF16),
            vm((CH, TOK), BF16),
            vm((8, TOK, EB), BF16),
            vm((4096, CH), BF16),
            vm((16, CH, OWN), BF16),
            vm((10, 2, QUART, OWN), BF16),
            vm((10, 2, HALF, OWN), BF16),
            vm((1024, 256), BF16),
            vm((64, 256), F32),
            vm((64, 256), F32),
            vm((128, 256), F32),
            vm((4, 4, 8, 128), F32),
            vm((3, 4, 8, 128), F32),
            vm((4, 8, 128), F32),
            vm((3, 8, 128), F32),
            pltpu.SemaphoreType.DMA((COPIES,)),
            pltpu.SemaphoreType.DMA((COPIES,)),
            pltpu.SemaphoreType.DMA((7,)),
        ],
        compiler_params=pltpu.CompilerParams(
            collective_id=0, has_side_effects=True, vmem_limit_bytes=53 * 1024 * 1024
        ),
        name="hyena_bwd",
    )(queries, keys, values, filters, grad_out, out_weight)
    gq, gk, gv, gf, gw = pl.pallas_call(
        store,
        out_shape=(
            jax.ShapeDtypeStruct((TOK, CH), BF16),
            jax.ShapeDtypeStruct((TOK, CH), BF16),
            jax.ShapeDtypeStruct((TOK, CH), BF16),
            jax.ShapeDtypeStruct((8, 64), F32),
            jax.ShapeDtypeStruct((OWN, CH), BF16),
        ),
        in_specs=[hbm] * 3 + [pl.BlockSpec(memory_space=vm)] * 2,
        out_specs=(hbm,) * 3 + (pl.BlockSpec(memory_space=vm),) * 2,
        scratch_shapes=[pltpu.SemaphoreType.DMA((3,))],
        compiler_params=pltpu.CompilerParams(vmem_limit_bytes=4 * 1024 * 1024),
        name="store",
    )(*out)
    return gq, gk, gv, gf.T, gw


def solution(mesh):
    return jax.shard_map(
        shards,
        mesh=mesh,
        in_specs=(
            P("seq", "ch"),
            P("seq", "ch"),
            P("seq", "ch"),
            P("ch", None),
            P("seq", "ch"),
            P("seq", "ch"),
        ),
        out_specs=(P("seq", "ch"), P("seq", "ch"), P("seq", "ch"), P("ch", "seq"), P("seq", "ch")),
        check_vma=False,
    )
```

```python
import jax
import jax.numpy as jnp
from jax import lax
from jax.experimental import pallas as pl
from jax.experimental.pallas import tpu as pltpu
from jax.sharding import PartitionSpec as P

F32 = jnp.float32
BF16 = jnp.bfloat16
MESH = pl.DeviceIdType.MESH
FILT = 128
TOK = 1024
CH = 1024
OWN = 256
EB = 512
HALF, QUART = 512, 256

W_COPIES, A_COPIES, R_COPIES = 32, 13, 40
A_BASE = W_COPIES
R_BASE = A_BASE + A_COPIES
H_BASE = R_BASE + R_COPIES
F_BASE = H_BASE + 2
COPIES = F_BASE + 6


def kernel(
    q_hbm, k_hbm, v_hbm, f_ref, a_hbm, w_hbm,
    mx, kb, vb, gfo, gwo,
    qb, pe, ge, gt, afull, wfull, part,
    bq, bf, tbl, rback, rahead, gfr, g1, r1, g2, r2,
    ssem, rsem, lsem,
):
    s = lax.axis_index("seq")
    h = lax.axis_index("ch")
    y, z = s // 4, s % 4
    xx, core = h // 2, h % 2

    def at(c, by):
        return (c + by + 4) % 4

    def dev_y(by):
        return (at(y, by) * 4 + z, h)

    def dev_z(by):
        return (y * 4 + at(z, by), h)

    def dev_x(by):
        return (s, at(xx, by) * 2 + core)

    sibling = (s, xx * 2 + (1 - core))
    after = ((s + 1) % 16, h)
    before = ((s + 15) % 16, h)

    sent = []

    def send(src, dst, k, dev):
        c = pltpu.make_async_remote_copy(
            src_ref=src, dst_ref=dst, send_sem=ssem.at[k], recv_sem=rsem.at[k],
            device_id=dev, device_id_type=MESH,
        )
        c.start()
        sent.append(c)

    def arrived(dst, k):
        pltpu.make_async_remote_copy(
            src_ref=dst, dst_ref=dst, send_sem=ssem.at[k], recv_sem=rsem.at[k],
            device_id=sibling, device_id_type=MESH,
        ).wait_recv()

    def local(src, dst, k):
        c = pltpu.make_async_copy(src, dst, lsem.at[k])
        c.start()
        return c

    own_w = wfull.at[pl.ds(pl.multiple_of(s * OWN, OWN), OWN)]
    tail, rest = pl.ds(TOK - FILT, FILT), pl.ds(0, TOK - FILT)
    ld_tail = [local(k_hbm.at[tail], kb.at[tail], 0), local(v_hbm.at[tail], vb.at[tail], 1)]
    ld_rest = [local(k_hbm.at[rest], kb.at[rest], 2), local(v_hbm.at[rest], vb.at[rest], 3)]
    ld_q = local(q_hbm, qb, 4)
    ld_w = local(w_hbm, own_w, 5)
    ld_a = local(a_hbm, afull.at[h], 6)

    peers = [dev_y(1), dev_y(2), dev_y(3), dev_z(1), dev_z(2), dev_z(3), dev_x(1), dev_x(3), sibling, after, before]
    bar = pltpu.get_barrier_semaphore()
    for p in peers:
        pl.semaphore_signal(bar, inc=1, device_id=p, device_id_type=MESH)

    def product_rows(r):
        rows = pl.ds(r, 128)
        pe[pl.ds(r + FILT, 128)] = (kb[rows].astype(F32) * vb[rows].astype(F32)).astype(BF16)

    for c in ld_tail:
        c.wait()
    product_rows(TOK - FILT)
    pl.semaphore_wait(bar, len(peers))
    send(pe.at[pl.ds(TOK, FILT)], pe.at[pl.ds(0, FILT)], H_BASE, after)

    def wrows(yy, zz, start, size):
        return wfull.at[pl.ds(pl.multiple_of((yy * 4 + zz) * OWN + start, 64), size)]

    for k, dev in ((0, dev_z(1)), (1, dev_z(-1)), (2, dev_y(1)), (3, dev_y(-1))):
        send(w_hbm, own_w, k, dev)

    def ablk(bx, bc, half=None):
        r = afull.at[at(xx, bx) * 2 + bc]
        return r if half is None else r.at[pl.ds(half * 512, 512)]

    own_lo, own_hi = ablk(0, core, 0), ablk(0, core, 1)
    send(a_hbm.at[pl.ds(0, 512)], own_lo, A_BASE + 0, dev_x(1))
    send(a_hbm.at[pl.ds(512, 512)], own_hi, A_BASE + 1, dev_x(-1))
    send(a_hbm.at[pl.ds(512, 512)], own_hi, A_BASE + 2, dev_x(1))
    send(a_hbm.at[pl.ds(0, 512)], own_lo, A_BASE + 3, dev_x(-1))
    send(a_hbm, ablk(0, core), A_BASE + 4, sibling)

    def w1_z_minus():
        arrived(wrows(y, at(z, -1), 0, 256), 0)
        r = wrows(y, at(z, -1), 0, 128)
        send(r, r, 4, dev_z(1))
        send(r, r, 8, dev_y(1))
        send(r, r, 9, dev_y(-1))

    def w1_z_plus():
        arrived(wrows(y, at(z, 1), 0, 256), 1)
        r = wrows(y, at(z, 1), 128, 128)
        send(r, r, 5, dev_z(-1))
        r = wrows(y, at(z, 1), 0, 128)
        send(r, r, 10, dev_y(1))
        send(r, r, 11, dev_y(-1))

    def w1_y_minus():
        arrived(wrows(at(y, -1), z, 0, 256), 2)
        r = wrows(at(y, -1), z, 0, 128)
        send(r, r, 6, dev_y(1))
        r = wrows(at(y, -1), z, 128, 128)
        send(r, r, 14, dev_z(1))
        send(r, r, 15, dev_z(-1))

    def w1_y_plus():
        arrived(wrows(at(y, 1), z, 0, 256), 3)
        r = wrows(at(y, 1), z, 128, 128)
        send(r, r, 7, dev_y(-1))
        send(r, r, 16, dev_z(1))
        send(r, r, 17, dev_z(-1))

    def w2_z():
        r = wrows(y, at(z, 2), 0, 128)
        arrived(r, 4)
        send(r, r, 12, dev_y(1))
        send(r, r, 13, dev_y(-1))

    def w2_y():
        r = wrows(at(y, 2), z, 128, 128)
        arrived(r, 7)
        send(r, r, 18, dev_z(1))
        send(r, r, 19, dev_z(-1))

    def w3(i, piece):
        bz = (-1, 1, 2)[i]
        if piece == 0:
            r = wrows(at(y, -1), at(z, bz), 0, 128)
            arrived(r, 8 + 2 * i)
            r = wrows(at(y, -1), at(z, bz), 0, 64)
            send(r, r, 20 + 2 * i, dev_y(1))
        elif piece == 1:
            r = wrows(at(y, 1), at(z, bz), 0, 128)
            arrived(r, 9 + 2 * i)
            r = wrows(at(y, 1), at(z, bz), 64, 64)
            send(r, r, 21 + 2 * i, dev_y(-1))
        elif piece == 2:
            r = wrows(at(y, bz), at(z, -1), 128, 128)
            arrived(r, 14 + 2 * i)
            r = wrows(at(y, bz), at(z, -1), 128, 64)
            send(r, r, 26 + 2 * i, dev_z(1))
        else:
            r = wrows(at(y, bz), at(z, 1), 128, 128)
            arrived(r, 15 + 2 * i)
            r = wrows(at(y, bz), at(z, 1), 192, 64)
            send(r, r, 27 + 2 * i, dev_z(-1))

    def w_last():
        arrived(wrows(y, at(z, 2), 128, 128), 5)
        arrived(wrows(at(y, 2), z, 0, 128), 6)
        for i in range(3):
            bz = (-1, 1, 2)[i]
            arrived(wrows(at(y, 2), at(z, bz), 0, 64), 20 + 2 * i)
            arrived(wrows(at(y, 2), at(z, bz), 64, 64), 21 + 2 * i)
            arrived(wrows(at(y, bz), at(z, 2), 128, 64), 26 + 2 * i)
            arrived(wrows(at(y, bz), at(z, 2), 192, 64), 27 + 2 * i)

    def near(bx, half, k):
        r = ablk(bx, core, half)
        arrived(r, A_BASE + k)
        if k < 2:
            send(r, r, A_BASE + 5 + k, dev_x(-bx))
        send(r, r, A_BASE + 7 + (0, 1, 2, 3)[k], sibling)

    def far(half):
        r = ablk(2, core, half)
        arrived(r, A_BASE + 5 + half)
        send(r, r, A_BASE + 11 + half, sibling)

    def from_sibling(bx):
        if bx == 0:
            arrived(ablk(0, 1 - core), A_BASE + 4)
            return
        lo, hi = {-1: (7, 9), 1: (10, 8), 2: (11, 12)}[bx]
        arrived(ablk(bx, 1 - core, 0), A_BASE + lo)
        arrived(ablk(bx, 1 - core, 1), A_BASE + hi)

    def rs_pieces(hf, stage, along_z, other):
        def chunk(by, q=None):
            idx = other * 4 + at(z, by) if along_z else at(y, by) * 4 + other
            if q is None:
                return part.at[idx, pl.ds(hf * HALF, HALF)]
            return part.at[idx, pl.ds(hf * HALF + q * QUART, QUART)]

        return chunk

    def rs(hf, stage, i):
        along_z = (hf == 0) == (stage == 0)
        other = at(y if along_z else z, i)
        dev = dev_z if along_z else dev_y
        chunk = rs_pieces(hf, stage, along_z, other)
        slot = hf * 5 + (i if stage == 0 else 4)
        base = R_BASE + slot * 4
        half_in = bq.at[slot]
        full_in = bf.at[slot]

        def start():
            send(chunk(2, 0), half_in.at[0], base + 0, dev(-1))
            send(chunk(2, 1), half_in.at[1], base + 1, dev(1))

        def mid(q):
            by = (-1, 1)[q]
            arrived(half_in.at[q], base + q)
            c = chunk(by, q)
            c[...] = (c[...].astype(F32) + half_in[q].astype(F32)).astype(BF16)
            send(chunk(by), full_in.at[q], base + 2 + q, dev(by))

        def fin():
            arrived(full_in.at[0], base + 2)
            arrived(full_in.at[1], base + 3)
            c = chunk(0)
            total = c[...].astype(F32) + full_in[0].astype(F32) + full_in[1].astype(F32)
            if stage == 0:
                c[...] = total.astype(BF16)
            else:
                gwo[hf * HALF : (hf + 1) * HALF] = total.astype(BF16)

        return start, mid, fin

    for c in ld_rest:
        c.wait()

    def product_loop(i, _):
        product_rows(pl.multiple_of(i * 128, 128))
        return 0

    lax.fori_loop(0, TOK // 128 - 1, product_loop, 0)

    tap = lax.broadcasted_iota(jnp.int32, (FILT, 256), 0)
    lane = lax.broadcasted_iota(jnp.int32, (FILT, 256), 1)
    f = f_ref[...]
    rback[...] = jnp.dot(f, (lane == FILT - tap).astype(F32).astype(BF16), preferred_element_type=F32)
    rahead[...] = jnp.dot(f, (lane == tap).astype(F32).astype(BF16), preferred_element_type=F32)
    group_of = (lane % 128) // 16

    def lanes_of(L):
        return pl.ds(pl.multiple_of(L * 128, 128), 128)

    def make_table(rows_ref, L):
        rows = rows_ref[pl.ds(pl.multiple_of(L * 8, 8), 8), :]
        for g in range(8):
            wide = jnp.broadcast_to(rows[g : g + 1, :], (FILT, 256))
            tbl[g * FILT : (g + 1) * FILT, :] = pltpu.roll(wide, 0, 1, stride=1, stride_axis=0).astype(BF16)

    def windows(ref, p, lanes):
        return jnp.concatenate([ref[pl.ds(p * 256, 256), lanes], ref[pl.ds(p * 256 + 128, 256), lanes]], axis=1)

    def filtered(ref, p, lanes):
        res = jnp.dot(tbl[...], windows(ref, p, lanes), preferred_element_type=F32)
        out = res[0:FILT]
        for g in range(1, 8):
            out = jnp.where(group_of == g, res[g * FILT : (g + 1) * FILT], out)
        return jnp.concatenate([out[:, :128], out[:, 128:]], axis=0)

    def conv_mixed(L, _):
        lanes = lanes_of(L)
        make_table(rback, L)
        for p in range(4):
            m = filtered(pe, p, lanes)
            rows = pl.ds(p * 256, 256)
            mx[rows, lanes] = m.astype(BF16)
            gated = (qb[rows, lanes].astype(F32) * m).astype(BF16)
            gt[lanes, rows] = gated.T
        return 0

    def prior_product():
        arrived(pe.at[pl.ds(0, FILT)], H_BASE)

        @pl.when(s == 0)
        def _():
            pe[pl.ds(0, FILT)] = jnp.zeros((FILT, CH), BF16)

        ld_q.wait()

    def weight_grad(bx, bc):
        blk = at(xx, bx) * 2 + bc

        def one(u, _):
            cols = pl.ds(pl.multiple_of(u * 256, 256), 256)
            r = jnp.dot(gt[...], afull[blk, :, cols], preferred_element_type=F32)
            part[blk * 2 + u] = r.astype(BF16)
            return 0

        lax.fori_loop(0, 2, one, 0)

    def rs_x(bx):
        return rs(0, 0, (xx + bx - y + 8) % 4)

    start, mid, fin = 0, 1, 2

    def gated_grad(n, _):
        cols = pl.ds(pl.multiple_of(n * 256, 256), 256)
        acc = jnp.dot(afull[0], wfull[pl.ds(0, EB), cols], preferred_element_type=F32)
        for b in range(1, 8):
            acc = acc + jnp.dot(afull[b], wfull[pl.ds(b * EB, EB), cols], preferred_element_type=F32)
        gg = acc.astype(BF16).astype(F32)
        ge[pl.ds(0, TOK), cols] = (gg * qb[:, cols].astype(F32)).astype(BF16)
        mx[:, cols] = (gg * mx[:, cols].astype(F32)).astype(BF16)
        return 0

    def send_mixed_halo():
        send(ge.at[pl.ds(0, FILT)], ge.at[pl.ds(TOK, FILT)], H_BASE + 1, before)

    flip = (lax.broadcasted_iota(jnp.int32, (FILT, FILT), 0) + lax.broadcasted_iota(jnp.int32, (FILT, FILT), 1) == FILT - 1)
    flip = flip.astype(F32).astype(BF16)

    def lag_products(L, _):
        lanes = lanes_of(L)
        acc = None
        for p in range(4):
            own = jnp.concatenate([ge[pl.ds(p * 256, 128), lanes], ge[pl.ds(p * 256 + 128, 128), lanes]], axis=1)
            own = jnp.dot(flip, own, preferred_element_type=F32)
            lhs = jnp.concatenate([jnp.where(group_of == g, own, 0.0).astype(BF16) for g in range(8)], axis=0)
            d = lax.dot_general(lhs, windows(pe, p, lanes), (((1,), (1,)), ((), ())), preferred_element_type=F32)
            acc = d if acc is None else acc + d
        sums = []
        for g in range(8):
            skew = pltpu.roll(acc[g * FILT : (g + 1) * FILT], 0, 1, stride=1, stride_axis=0)
            sums.append(jnp.sum(skew, axis=0, keepdims=True))
        gfr[pl.ds(pl.multiple_of(L * 8, 8), 8), :] = jnp.concatenate(sums, axis=0)
        return 0

    def send_taps_z():
        pick = (lane == 255 - tap).astype(F32).astype(BF16)
        hi = gfr[...].astype(BF16)
        lo = (gfr[...] - hi.astype(F32)).astype(BF16)
        nt = (((1,), (1,)), ((), ()))
        taps = lax.dot_general(pick, hi, nt, preferred_element_type=F32)
        taps = taps + lax.dot_general(pick, lo, nt, preferred_element_type=F32)
        for i in range(16):
            g1[i % 4, i // 4] = taps[i * 8 : (i + 1) * 8]
        for d in (1, 2, 3):
            send(g1.at[at(z, d)], r1.at[d - 1], F_BASE + d - 1, dev_z(d))

    def send_taps_y():
        for d in (1, 2, 3):
            arrived(r1.at[d - 1], F_BASE + d - 1)
        g2[...] = g1[z] + r1[0] + r1[1] + r1[2]
        for d in (1, 2, 3):
            send(g2.at[at(y, d)], r2.at[d - 1], F_BASE + 2 + d, dev_y(d))

    def sum_taps():
        for d in (1, 2, 3):
            arrived(r2.at[d - 1], F_BASE + 2 + d)
        gfo[...] = g2[y] + r2[0] + r2[1] + r2[2]

    def later_mixed():
        arrived(ge.at[pl.ds(TOK, FILT)], H_BASE + 1)

        @pl.when(s == 15)
        def _():
            ge[pl.ds(TOK, FILT)] = jnp.zeros((FILT, CH), BF16)

    def conv_grad(L, _):
        lanes = lanes_of(L)
        make_table(rahead, L)
        for p in range(4):
            m = filtered(ge, p, lanes)
            rows = pl.ds(p * 256, 256)
            keys, values = kb[rows, lanes].astype(F32), vb[rows, lanes].astype(F32)
            kb[rows, lanes] = (m * values).astype(BF16)
            vb[rows, lanes] = (m * keys).astype(BF16)
        return 0

    ld_w.wait()
    w1_y_minus()
    w1_y_plus()
    prior_product()
    lax.fori_loop(0, 2, conv_mixed, 0)
    near(1, 1, 1)
    lax.fori_loop(2, 3, conv_mixed, 0)
    w1_z_plus()
    lax.fori_loop(3, 4, conv_mixed, 0)
    w1_z_minus()
    lax.fori_loop(4, 6, conv_mixed, 0)
    near(-1, 0, 0)
    w2_y()
    lax.fori_loop(6, 7, conv_mixed, 0)
    near(-1, 1, 2)
    lax.fori_loop(7, 8, conv_mixed, 0)
    near(1, 0, 3)
    ld_a.wait()
    weight_grad(0, core)
    from_sibling(-1)
    weight_grad(-1, 1 - core)
    w3(1, 0)
    w3(1, 1)
    w3(1, 3)
    weight_grad(-1, core)
    w2_z()
    rs_x(-1)[start]()
    weight_grad(1, core)
    w3(0, 1)
    w3(1, 2)
    far(1)
    w3(2, 3)
    w3(0, 0)
    from_sibling(1)
    weight_grad(1, 1 - core)
    far(0)
    w3(0, 3)
    w3(2, 2)
    from_sibling(0)
    weight_grad(0, 1 - core)
    w3(0, 2)
    w3(2, 1)
    w3(2, 0)
    rs_x(1)[start]()
    from_sibling(2)
    weight_grad(2, 1 - core)
    weight_grad(2, core)
    rs(1, 0, 1)[start]()
    rs(1, 0, 2)[start]()
    rs_x(2)[start]()
    rs_x(0)[start]()
    w_last()
    rs(1, 0, 0)[start]()
    rs_x(-1)[mid](0)
    rs(1, 0, 3)[start]()
    rs_x(1)[mid](0)
    rs(1, 0, 1)[mid](1)
    lax.fori_loop(0, 1, gated_grad, 0)
    rs(1, 0, 1)[mid](0)
    rs_x(-1)[mid](1)
    lax.fori_loop(1, 2, gated_grad, 0)
    rs(1, 0, 2)[mid](0)
    rs_x(2)[mid](1)
    rs(1, 0, 0)[mid](0)
    lax.fori_loop(2, 3, gated_grad, 0)
    rs_x(2)[mid](0)
    rs(1, 0, 2)[mid](1)
    rs(1, 0, 0)[mid](1)
    rs_x(0)[mid](1)
    lax.fori_loop(3, 4, gated_grad, 0)
    rs_x(0)[mid](0)
    send_mixed_halo()
    gfr[...] = jnp.zeros((128, 256), F32)
    lax.fori_loop(0, 2, lag_products, 0)
    rs_x(1)[mid](1)
    rs(1, 0, 3)[mid](0)
    rs(1, 0, 2)[fin]()
    lax.fori_loop(2, 4, lag_products, 0)
    rs(1, 0, 3)[mid](1)
    rs(1, 0, 1)[fin]()
    lax.fori_loop(4, 8, lag_products, 0)
    send_taps_z()
    rs(1, 1, 0)[start]()
    rs(0, 0, 3)[fin]()
    rs(0, 0, 2)[fin]()
    rs(0, 1, 0)[start]()
    rs(1, 0, 0)[fin]()
    rs(0, 0, 1)[fin]()
    later_mixed()
    lax.fori_loop(0, 1, conv_grad, 0)
    rs(1, 0, 3)[fin]()
    lax.fori_loop(1, 2, conv_grad, 0)
    rs(1, 1, 0)[mid](1)
    rs(1, 1, 0)[mid](0)
    send_taps_y()
    rs(0, 1, 0)[mid](1)
    rs(0, 1, 0)[mid](0)
    lax.fori_loop(2, 5, conv_grad, 0)
    sum_taps()
    rs(0, 0, 0)[fin]()
    lax.fori_loop(5, 8, conv_grad, 0)
    rs(1, 1, 0)[fin]()
    rs(0, 1, 0)[fin]()
    for c in sent:
        c.wait_send()


def store(gq, gk, gv, gf, gw, gq_out, gk_out, gv_out, gf_out, gw_out, sem):
    copies = [
        pltpu.make_async_copy(src, dst, sem.at[i])
        for i, (src, dst) in enumerate(((gq, gq_out), (gk, gk_out), (gv, gv_out)))
    ]
    for c in copies:
        c.start()
    gw_out[...] = gw[...].T
    gf_out[...] = gf[:, :64]
    for c in copies:
        c.wait()


def shards(queries, keys, values, filters, grad_out, out_weight):
    hbm = pl.BlockSpec(memory_space=pl.ANY)
    vm = pltpu.VMEM
    out = pl.pallas_call(
        kernel,
        out_shape=(
            vm((TOK, CH), BF16),
            vm((TOK, CH), BF16),
            vm((TOK, CH), BF16),
            vm((8, 128), F32),
            vm((CH, OWN), BF16),
        ),
        in_specs=[hbm, hbm, hbm, pl.BlockSpec(memory_space=pltpu.VMEM), hbm, hbm],
        out_specs=(pl.BlockSpec(memory_space=pltpu.VMEM),) * 5,
        scratch_shapes=[
            vm((TOK, CH), BF16),
            vm((TOK + FILT, CH), BF16),
            vm((TOK + FILT, CH), BF16),
            vm((CH, TOK), BF16),
            vm((8, TOK, EB), BF16),
            vm((4096, CH), BF16),
            vm((16, CH, OWN), BF16),
            vm((10, 2, QUART, OWN), BF16),
            vm((10, 2, HALF, OWN), BF16),
            vm((1024, 256), BF16),
            vm((64, 256), F32),
            vm((64, 256), F32),
            vm((128, 256), F32),
            vm((4, 4, 8, 128), F32),
            vm((3, 4, 8, 128), F32),
            vm((4, 8, 128), F32),
            vm((3, 8, 128), F32),
            pltpu.SemaphoreType.DMA((COPIES,)),
            pltpu.SemaphoreType.DMA((COPIES,)),
            pltpu.SemaphoreType.DMA((7,)),
        ],
        compiler_params=pltpu.CompilerParams(
            collective_id=0, has_side_effects=True, vmem_limit_bytes=53 * 1024 * 1024
        ),
        name="hyena_bwd",
    )(queries, keys, values, filters, grad_out, out_weight)
    gq, gk, gv, gf, gw = pl.pallas_call(
        store,
        out_shape=(
            jax.ShapeDtypeStruct((TOK, CH), BF16),
            jax.ShapeDtypeStruct((TOK, CH), BF16),
            jax.ShapeDtypeStruct((TOK, CH), BF16),
            jax.ShapeDtypeStruct((8, 64), F32),
            jax.ShapeDtypeStruct((OWN, CH), BF16),
        ),
        in_specs=[hbm] * 3 + [pl.BlockSpec(memory_space=vm)] * 2,
        out_specs=(hbm,) * 3 + (pl.BlockSpec(memory_space=vm),) * 2,
        scratch_shapes=[pltpu.SemaphoreType.DMA((3,))],
        compiler_params=pltpu.CompilerParams(vmem_limit_bytes=4 * 1024 * 1024),
        name="store",
    )(*out)
    return gq, gk, gv, gf.T, gw


def solution(mesh):
    return jax.shard_map(
        shards,
        mesh=mesh,
        in_specs=(
            P("seq", "ch"),
            P("seq", "ch"),
            P("seq", "ch"),
            P("ch", None),
            P("seq", "ch"),
            P("seq", "ch"),
        ),
        out_specs=(P("seq", "ch"), P("seq", "ch"), P("seq", "ch"), P("ch", "seq"), P("seq", "ch")),
        check_vma=False,
    )
```

```python
import jax
import jax.numpy as jnp
from jax import lax
from jax.experimental import pallas as pl
from jax.experimental.pallas import tpu as pltpu
from jax.sharding import PartitionSpec as P

F32 = jnp.float32
BF16 = jnp.bfloat16
MESH = pl.DeviceIdType.MESH
FILT = 128
TOK = 1024
CH = 1024
OWN = 256
EB = 512
SPLIT = (0, 448)
QUART = (224, 288)

W_COPIES, A_COPIES, R_COPIES = 32, 13, 60
A_BASE = W_COPIES
R_BASE = A_BASE + A_COPIES
H_BASE = R_BASE + R_COPIES
F_BASE = H_BASE + 2
COPIES = F_BASE + 6


def kernel(
    q_hbm, k_hbm, v_hbm, f_ref, a_hbm, w_hbm,
    mx, kb, vb, gfo, gwo,
    qb, pe, ge, gt, afull, wfull, part,
    boxes, tbl, rback, rahead, gfr, g1, r1, g2, r2,
    ssem, rsem, lsem,
):
    s = lax.axis_index("seq")
    h = lax.axis_index("ch")
    y, z = s // 4, s % 4
    xx, core = h // 2, h % 2

    def at(c, by):
        return (c + by + 4) % 4

    def dev_y(by):
        return (at(y, by) * 4 + z, h)

    def dev_z(by):
        return (y * 4 + at(z, by), h)

    def dev_x(by):
        return (s, at(xx, by) * 2 + core)

    sibling = (s, xx * 2 + (1 - core))
    after = ((s + 1) % 16, h)
    before = ((s + 15) % 16, h)

    sent = []

    def send(src, dst, k, dev):
        c = pltpu.make_async_remote_copy(
            src_ref=src, dst_ref=dst, send_sem=ssem.at[k], recv_sem=rsem.at[k],
            device_id=dev, device_id_type=MESH,
        )
        c.start()
        sent.append(c)

    def arrived(dst, k):
        pltpu.make_async_remote_copy(
            src_ref=dst, dst_ref=dst, send_sem=ssem.at[k], recv_sem=rsem.at[k],
            device_id=sibling, device_id_type=MESH,
        ).wait_recv()

    def local(src, dst, k):
        c = pltpu.make_async_copy(src, dst, lsem.at[k])
        c.start()
        return c

    peers = [dev_y(1), dev_y(2), dev_y(3), dev_z(1), dev_z(2), dev_z(3), dev_x(1), dev_x(3), sibling, after, before]
    bar = pltpu.get_barrier_semaphore()
    for p in peers:
        pl.semaphore_signal(bar, inc=1, device_id=p, device_id_type=MESH)

    own_w = wfull.at[pl.ds(pl.multiple_of(s * OWN, OWN), OWN)]
    tail, rest = pl.ds(TOK - FILT, FILT), pl.ds(0, TOK - FILT)
    ld_tail = [local(k_hbm.at[tail], kb.at[tail], 0), local(v_hbm.at[tail], vb.at[tail], 1)]
    ld_rest = [local(k_hbm.at[rest], kb.at[rest], 2), local(v_hbm.at[rest], vb.at[rest], 3)]
    ld_q = local(q_hbm, qb, 4)
    ld_w = local(w_hbm, own_w, 5)
    ld_a = local(a_hbm, afull.at[h], 6)

    def product_rows(r):
        rows = pl.ds(r, 128)
        pe[pl.ds(r + FILT, 128)] = (kb[rows].astype(F32) * vb[rows].astype(F32)).astype(BF16)

    for c in ld_tail:
        c.wait()
    product_rows(TOK - FILT)
    pl.semaphore_wait(bar, len(peers))
    send(pe.at[pl.ds(TOK, FILT)], pe.at[pl.ds(0, FILT)], H_BASE, after)

    def wrows(yy, zz, start, size):
        return wfull.at[pl.ds(pl.multiple_of((yy * 4 + zz) * OWN + start, 64), size)]

    for k, dev in ((0, dev_z(1)), (1, dev_z(-1)), (2, dev_y(1)), (3, dev_y(-1))):
        send(w_hbm, own_w, k, dev)

    def ablk(bx, bc, half=None):
        r = afull.at[at(xx, bx) * 2 + bc]
        return r if half is None else r.at[pl.ds(half * 512, 512)]

    own_lo, own_hi = ablk(0, core, 0), ablk(0, core, 1)
    send(a_hbm.at[pl.ds(0, 512)], own_lo, A_BASE + 0, dev_x(1))
    send(a_hbm.at[pl.ds(512, 512)], own_hi, A_BASE + 1, dev_x(-1))
    send(a_hbm.at[pl.ds(512, 512)], own_hi, A_BASE + 2, dev_x(1))
    send(a_hbm.at[pl.ds(0, 512)], own_lo, A_BASE + 3, dev_x(-1))
    send(a_hbm, ablk(0, core), A_BASE + 4, sibling)

    def w1_z_minus():
        arrived(wrows(y, at(z, -1), 0, 256), 0)
        r = wrows(y, at(z, -1), 0, 128)
        send(r, r, 4, dev_z(1))
        send(r, r, 8, dev_y(1))
        send(r, r, 9, dev_y(-1))

    def w1_z_plus():
        arrived(wrows(y, at(z, 1), 0, 256), 1)
        r = wrows(y, at(z, 1), 128, 128)
        send(r, r, 5, dev_z(-1))
        r = wrows(y, at(z, 1), 0, 128)
        send(r, r, 10, dev_y(1))
        send(r, r, 11, dev_y(-1))

    def w1_y_minus():
        arrived(wrows(at(y, -1), z, 0, 256), 2)
        r = wrows(at(y, -1), z, 0, 128)
        send(r, r, 6, dev_y(1))
        r = wrows(at(y, -1), z, 128, 128)
        send(r, r, 14, dev_z(1))
        send(r, r, 15, dev_z(-1))

    def w1_y_plus():
        arrived(wrows(at(y, 1), z, 0, 256), 3)
        r = wrows(at(y, 1), z, 128, 128)
        send(r, r, 7, dev_y(-1))
        send(r, r, 16, dev_z(1))
        send(r, r, 17, dev_z(-1))

    def w2_z():
        r = wrows(y, at(z, 2), 0, 128)
        arrived(r, 4)
        send(r, r, 12, dev_y(1))
        send(r, r, 13, dev_y(-1))

    def w2_y():
        r = wrows(at(y, 2), z, 128, 128)
        arrived(r, 7)
        send(r, r, 18, dev_z(1))
        send(r, r, 19, dev_z(-1))

    def w3(i, piece):
        bz = (-1, 1, 2)[i]
        if piece == 0:
            r = wrows(at(y, -1), at(z, bz), 0, 128)
            arrived(r, 8 + 2 * i)
            r = wrows(at(y, -1), at(z, bz), 0, 64)
            send(r, r, 20 + 2 * i, dev_y(1))
        elif piece == 1:
            r = wrows(at(y, 1), at(z, bz), 0, 128)
            arrived(r, 9 + 2 * i)
            r = wrows(at(y, 1), at(z, bz), 64, 64)
            send(r, r, 21 + 2 * i, dev_y(-1))
        elif piece == 2:
            r = wrows(at(y, bz), at(z, -1), 128, 128)
            arrived(r, 14 + 2 * i)
            r = wrows(at(y, bz), at(z, -1), 128, 64)
            send(r, r, 26 + 2 * i, dev_z(1))
        else:
            r = wrows(at(y, bz), at(z, 1), 128, 128)
            arrived(r, 15 + 2 * i)
            r = wrows(at(y, bz), at(z, 1), 192, 64)
            send(r, r, 27 + 2 * i, dev_z(-1))

    def w_last():
        arrived(wrows(y, at(z, 2), 128, 128), 5)
        arrived(wrows(at(y, 2), z, 0, 128), 6)
        for i in range(3):
            bz = (-1, 1, 2)[i]
            arrived(wrows(at(y, 2), at(z, bz), 0, 64), 20 + 2 * i)
            arrived(wrows(at(y, 2), at(z, bz), 64, 64), 21 + 2 * i)
            arrived(wrows(at(y, bz), at(z, 2), 128, 64), 26 + 2 * i)
            arrived(wrows(at(y, bz), at(z, 2), 192, 64), 27 + 2 * i)

    def near(bx, half, k):
        r = ablk(bx, core, half)
        arrived(r, A_BASE + k)
        if k < 2:
            send(r, r, A_BASE + 5 + k, dev_x(-bx))
        send(r, r, A_BASE + 7 + (0, 1, 2, 3)[k], sibling)

    def far(half):
        r = ablk(2, core, half)
        arrived(r, A_BASE + 5 + half)
        send(r, r, A_BASE + 11 + half, sibling)

    def from_sibling(bx):
        if bx == 0:
            arrived(ablk(0, 1 - core), A_BASE + 4)
            return
        lo, hi = {-1: (7, 9), 1: (10, 8), 2: (11, 12)}[bx]
        arrived(ablk(bx, 1 - core, 0), A_BASE + lo)
        arrived(ablk(bx, 1 - core, 1), A_BASE + hi)

    def rs(hf, stage, i):
        along_z = (hf == 0) == (stage == 0)
        other = at(y if along_z else z, i)
        dev = dev_z if along_z else dev_y
        slot = hf * 5 + (i if stage == 0 else 4)
        base = R_BASE + slot * 6
        size = QUART[hf]

        def chunk(by, q):
            idx = other * 4 + at(z, by) if along_z else at(y, by) * 4 + other
            return part.at[idx, pl.ds(SPLIT[hf] + q * size, size)]

        def box(kind, q):
            return boxes.at[slot, kind * 2 + q, pl.ds(0, size)]

        def direct(q):
            by = (-1, 1)[q]
            send(chunk(by, 1 - q), box(1, q), base + 2 + q, dev(by))

        def start():
            send(chunk(2, 0), box(0, 0), base + 0, dev(-1))
            send(chunk(2, 1), box(0, 1), base + 1, dev(1))
            if stage == 0:
                direct(0)
                direct(1)

        def mid(q):
            by = (-1, 1)[q]
            arrived(box(0, q), base + q)
            c = chunk(by, q)
            c[...] = (c[...].astype(F32) + box(0, q)[...].astype(F32)).astype(BF16)
            send(c, box(2, q), base + 4 + q, dev(by))

        def fin():
            for kind in (1, 2):
                for q in (0, 1):
                    arrived(box(kind, q), base + 2 * kind + q)
            for q in (0, 1):
                c = chunk(0, q)
                total = c[...].astype(F32) + box(1, 1 - q)[...].astype(F32) + box(2, q)[...].astype(F32)
                if stage == 0:
                    c[...] = total.astype(BF16)
                else:
                    gwo[SPLIT[hf] + q * size : SPLIT[hf] + (q + 1) * size] = total.astype(BF16)

        return start, mid, fin, direct

    for c in ld_rest:
        c.wait()

    def product_loop(i, _):
        product_rows(pl.multiple_of(i * 128, 128))
        return 0

    lax.fori_loop(0, TOK // 128 - 1, product_loop, 0)

    tap = lax.broadcasted_iota(jnp.int32, (FILT, 256), 0)
    lane = lax.broadcasted_iota(jnp.int32, (FILT, 256), 1)
    f = f_ref[...]
    rback[...] = jnp.dot(f, (lane == FILT - tap).astype(F32).astype(BF16), preferred_element_type=F32)
    rahead[...] = jnp.dot(f, (lane == tap).astype(F32).astype(BF16), preferred_element_type=F32)
    group_of = (lane % 128) // 16

    def lanes_of(L):
        return pl.ds(pl.multiple_of(L * 128, 128), 128)

    def make_table(rows_ref, L):
        rows = rows_ref[pl.ds(pl.multiple_of(L * 8, 8), 8), :]
        for g in range(8):
            wide = jnp.broadcast_to(rows[g : g + 1, :], (FILT, 256))
            tbl[g * FILT : (g + 1) * FILT, :] = pltpu.roll(wide, 0, 1, stride=1, stride_axis=0).astype(BF16)

    def windows(ref, p, lanes):
        return jnp.concatenate([ref[pl.ds(p * 256, 256), lanes], ref[pl.ds(p * 256 + 128, 256), lanes]], axis=1)

    def filtered(ref, p, lanes):
        res = jnp.dot(tbl[...], windows(ref, p, lanes), preferred_element_type=F32)
        out = res[0:FILT]
        for g in range(1, 8):
            out = jnp.where(group_of == g, res[g * FILT : (g + 1) * FILT], out)
        return jnp.concatenate([out[:, :128], out[:, 128:]], axis=0)

    def conv_mixed(L, _):
        lanes = lanes_of(L)
        make_table(rback, L)
        for p in range(4):
            m = filtered(pe, p, lanes)
            rows = pl.ds(p * 256, 256)
            mx[rows, lanes] = m.astype(BF16)
            gated = (qb[rows, lanes].astype(F32) * m).astype(BF16)
            gt[lanes, rows] = gated.T
        return 0

    def prior_product():
        arrived(pe.at[pl.ds(0, FILT)], H_BASE)

        @pl.when(s == 0)
        def _():
            pe[pl.ds(0, FILT)] = jnp.zeros((FILT, CH), BF16)

        ld_q.wait()

    def weight_grad(bx, bc):
        blk = at(xx, bx) * 2 + bc

        def one(u, _):
            cols = pl.ds(pl.multiple_of(u * 256, 256), 256)
            r = jnp.dot(gt[...], afull[blk, :, cols], preferred_element_type=F32)
            part[blk * 2 + u] = r.astype(BF16)
            return 0

        lax.fori_loop(0, 2, one, 0)

    def rs_x(bx):
        return rs(0, 0, (xx + bx - y + 8) % 4)

    start, mid, fin, direct = 0, 1, 2, 3

    def gated_grad(n, _):
        cols = pl.ds(pl.multiple_of(n * 256, 256), 256)
        acc = jnp.dot(afull[0], wfull[pl.ds(0, EB), cols], preferred_element_type=F32)
        for b in range(1, 8):
            acc = acc + jnp.dot(afull[b], wfull[pl.ds(b * EB, EB), cols], preferred_element_type=F32)
        gg = acc.astype(BF16).astype(F32)
        ge[pl.ds(0, TOK), cols] = (gg * qb[:, cols].astype(F32)).astype(BF16)
        mx[:, cols] = (gg * mx[:, cols].astype(F32)).astype(BF16)
        return 0

    def send_mixed_halo():
        send(ge.at[pl.ds(0, FILT)], ge.at[pl.ds(TOK, FILT)], H_BASE + 1, before)

    flip = (lax.broadcasted_iota(jnp.int32, (FILT, FILT), 0) + lax.broadcasted_iota(jnp.int32, (FILT, FILT), 1) == FILT - 1)
    flip = flip.astype(F32).astype(BF16)

    def lag_products(L, _):
        lanes = lanes_of(L)
        acc = None
        for p in range(4):
            own = jnp.concatenate([ge[pl.ds(p * 256, 128), lanes], ge[pl.ds(p * 256 + 128, 128), lanes]], axis=1)
            own = jnp.dot(flip, own, preferred_element_type=F32)
            lhs = jnp.concatenate([jnp.where(group_of == g, own, 0.0).astype(BF16) for g in range(8)], axis=0)
            d = lax.dot_general(lhs, windows(pe, p, lanes), (((1,), (1,)), ((), ())), preferred_element_type=F32)
            acc = d if acc is None else acc + d
        sums = []
        for g in range(8):
            skew = pltpu.roll(acc[g * FILT : (g + 1) * FILT], 0, 1, stride=1, stride_axis=0)
            sums.append(jnp.sum(skew, axis=0, keepdims=True))
        gfr[pl.ds(pl.multiple_of(L * 8, 8), 8), :] = jnp.concatenate(sums, axis=0)
        return 0

    def send_taps_z():
        pick = (lane == 255 - tap).astype(F32).astype(BF16)
        hi = gfr[...].astype(BF16)
        lo = (gfr[...] - hi.astype(F32)).astype(BF16)
        nt = (((1,), (1,)), ((), ()))
        taps = lax.dot_general(pick, hi, nt, preferred_element_type=F32)
        taps = taps + lax.dot_general(pick, lo, nt, preferred_element_type=F32)
        for i in range(16):
            g1[i % 4, i // 4] = taps[i * 8 : (i + 1) * 8]
        for d in (1, 2, 3):
            send(g1.at[at(z, d)], r1.at[d - 1], F_BASE + d - 1, dev_z(d))

    def send_taps_y():
        for d in (1, 2, 3):
            arrived(r1.at[d - 1], F_BASE + d - 1)
        g2[...] = g1[z] + r1[0] + r1[1] + r1[2]
        for d in (1, 2, 3):
            send(g2.at[at(y, d)], r2.at[d - 1], F_BASE + 2 + d, dev_y(d))

    def sum_taps():
        for d in (1, 2, 3):
            arrived(r2.at[d - 1], F_BASE + 2 + d)
        gfo[...] = g2[y] + r2[0] + r2[1] + r2[2]

    def later_mixed():
        arrived(ge.at[pl.ds(TOK, FILT)], H_BASE + 1)

        @pl.when(s == 15)
        def _():
            ge[pl.ds(TOK, FILT)] = jnp.zeros((FILT, CH), BF16)

    def conv_grad(L, _):
        lanes = lanes_of(L)
        make_table(rahead, L)
        for p in range(4):
            m = filtered(ge, p, lanes)
            rows = pl.ds(p * 256, 256)
            keys, values = kb[rows, lanes].astype(F32), vb[rows, lanes].astype(F32)
            kb[rows, lanes] = (m * values).astype(BF16)
            vb[rows, lanes] = (m * keys).astype(BF16)
        return 0

    ld_w.wait()
    w1_y_plus()
    w1_z_plus()
    prior_product()
    lax.fori_loop(0, 3, conv_mixed, 0)
    w1_z_minus()
    near(-1, 0, 0)
    lax.fori_loop(3, 4, conv_mixed, 0)
    w1_y_minus()
    near(1, 1, 1)
    lax.fori_loop(4, 6, conv_mixed, 0)
    near(-1, 1, 2)
    lax.fori_loop(6, 7, conv_mixed, 0)
    w2_y()
    lax.fori_loop(7, 8, conv_mixed, 0)
    ld_a.wait()
    weight_grad(0, core)
    near(1, 0, 3)
    w3(1, 3)
    w3(1, 1)
    w2_z()
    w3(0, 0)
    from_sibling(-1)
    weight_grad(-1, 1 - core)
    w3(1, 0)
    w3(1, 2)
    weight_grad(-1, core)
    from_sibling(0)
    weight_grad(0, 1 - core)
    far(1)
    from_sibling(1)
    weight_grad(1, 1 - core)
    w3(0, 3)
    w3(0, 2)
    w3(0, 1)
    w3(2, 3)
    far(0)
    w3(2, 0)
    weight_grad(2, core)
    w3(2, 1)
    weight_grad(1, core)
    w3(2, 2)
    rs_x(-1)[start]()
    from_sibling(2)
    weight_grad(2, 1 - core)
    rs(1, 0, 3)[start]()
    rs_x(1)[start]()
    rs_x(0)[start]()
    rs(1, 0, 2)[start]()
    rs(1, 0, 1)[start]()
    w_last()
    lax.fori_loop(0, 1, gated_grad, 0)
    rs_x(1)[mid](0)
    lax.fori_loop(1, 3, gated_grad, 0)
    rs(1, 0, 2)[mid](0)
    lax.fori_loop(3, 4, gated_grad, 0)
    gfr[...] = jnp.zeros((128, 256), F32)
    lax.fori_loop(0, 1, lag_products, 0)
    send_mixed_halo()
    rs(1, 0, 0)[start]()
    lax.fori_loop(1, 2, lag_products, 0)
    rs(1, 0, 3)[mid](0)
    rs_x(2)[start]()
    lax.fori_loop(2, 4, lag_products, 0)
    rs(1, 0, 2)[mid](1)
    lax.fori_loop(4, 5, lag_products, 0)
    rs(1, 0, 3)[mid](1)
    lax.fori_loop(5, 6, lag_products, 0)
    rs_x(-1)[mid](1)
    rs(1, 0, 1)[mid](0)
    lax.fori_loop(6, 7, lag_products, 0)
    rs(1, 0, 1)[mid](1)
    rs_x(0)[mid](1)
    rs_x(2)[mid](1)
    later_mixed()
    lax.fori_loop(0, 1, conv_grad, 0)
    rs(1, 0, 0)[mid](1)
    rs_x(0)[mid](0)
    lax.fori_loop(7, 8, lag_products, 0)
    rs_x(2)[mid](0)
    rs(1, 0, 0)[mid](0)
    lax.fori_loop(1, 2, conv_grad, 0)
    rs_x(-1)[mid](0)
    lax.fori_loop(2, 3, conv_grad, 0)
    rs_x(1)[mid](1)
    rs(1, 0, 2)[fin]()
    lax.fori_loop(3, 4, conv_grad, 0)
    rs(1, 1, 0)[start]()
    lax.fori_loop(4, 6, conv_grad, 0)
    send_taps_z()
    rs(1, 0, 3)[fin]()
    lax.fori_loop(6, 7, conv_grad, 0)
    rs(0, 0, 2)[fin]()
    rs(0, 1, 0)[start]()
    rs(0, 0, 1)[fin]()
    rs(1, 0, 1)[fin]()
    rs(1, 1, 0)[direct](1)
    rs(0, 1, 0)[direct](1)
    rs(0, 0, 3)[fin]()
    rs(1, 1, 0)[direct](0)
    rs(0, 1, 0)[direct](0)
    rs(0, 0, 0)[fin]()
    rs(1, 1, 0)[mid](0)
    rs(1, 1, 0)[mid](1)
    send_taps_y()
    rs(0, 1, 0)[mid](0)
    rs(0, 1, 0)[mid](1)
    rs(1, 0, 0)[fin]()
    lax.fori_loop(7, 8, conv_grad, 0)
    sum_taps()
    rs(1, 1, 0)[fin]()
    rs(0, 1, 0)[fin]()
    for c in sent:
        c.wait_send()


def store(gq, gk, gv, gf, gw, gq_out, gk_out, gv_out, gf_out, gw_out, sem):
    copies = [
        pltpu.make_async_copy(src.at[pl.ds(r * 256, 256)], dst.at[pl.ds(r * 256, 256)], sem.at[i, r])
        for r in range(4)
        for i, (src, dst) in enumerate(((gq, gq_out), (gk, gk_out), (gv, gv_out)))
    ]
    for c in copies:
        c.start()
    gw_out[...] = gw[...].T
    gf_out[...] = gf[:, :64]
    for c in copies:
        c.wait()


def shards(queries, keys, values, filters, grad_out, out_weight):
    hbm = pl.BlockSpec(memory_space=pl.ANY)
    vm = pltpu.VMEM
    out = pl.pallas_call(
        kernel,
        out_shape=(
            vm((TOK, CH), BF16),
            vm((TOK, CH), BF16),
            vm((TOK, CH), BF16),
            vm((8, 128), F32),
            vm((CH, OWN), BF16),
        ),
        in_specs=[hbm, hbm, hbm, pl.BlockSpec(memory_space=pltpu.VMEM), hbm, hbm],
        out_specs=(pl.BlockSpec(memory_space=pltpu.VMEM),) * 5,
        scratch_shapes=[
            vm((TOK, CH), BF16),
            vm((TOK + FILT, CH), BF16),
            vm((TOK + FILT, CH), BF16),
            vm((CH, TOK), BF16),
            vm((8, TOK, EB), BF16),
            vm((4096, CH), BF16),
            vm((16, CH, OWN), BF16),
            vm((10, 6, max(QUART), OWN), BF16),
            vm((1024, 256), BF16),
            vm((64, 256), F32),
            vm((64, 256), F32),
            vm((128, 256), F32),
            vm((4, 4, 8, 128), F32),
            vm((3, 4, 8, 128), F32),
            vm((4, 8, 128), F32),
            vm((3, 8, 128), F32),
            pltpu.SemaphoreType.DMA((COPIES,)),
            pltpu.SemaphoreType.DMA((COPIES,)),
            pltpu.SemaphoreType.DMA((7,)),
        ],
        compiler_params=pltpu.CompilerParams(
            collective_id=0, has_side_effects=True, vmem_limit_bytes=53 * 1024 * 1024
        ),
        name="hyena_bwd",
    )(queries, keys, values, filters, grad_out, out_weight)
    gq, gk, gv, gf, gw = pl.pallas_call(
        store,
        out_shape=(
            jax.ShapeDtypeStruct((TOK, CH), BF16),
            jax.ShapeDtypeStruct((TOK, CH), BF16),
            jax.ShapeDtypeStruct((TOK, CH), BF16),
            jax.ShapeDtypeStruct((8, 64), F32),
            jax.ShapeDtypeStruct((OWN, CH), BF16),
        ),
        in_specs=[hbm] * 3 + [pl.BlockSpec(memory_space=vm)] * 2,
        out_specs=(hbm,) * 3 + (pl.BlockSpec(memory_space=vm),) * 2,
        scratch_shapes=[pltpu.SemaphoreType.DMA((3, 4))],
        compiler_params=pltpu.CompilerParams(vmem_limit_bytes=4 * 1024 * 1024),
        name="store",
    )(*out)
    return gq, gk, gv, gf.T, gw


def solution(mesh):
    return jax.shard_map(
        shards,
        mesh=mesh,
        in_specs=(
            P("seq", "ch"),
            P("seq", "ch"),
            P("seq", "ch"),
            P("ch", None),
            P("seq", "ch"),
            P("seq", "ch"),
        ),
        out_specs=(P("seq", "ch"), P("seq", "ch"), P("seq", "ch"), P("ch", "seq"), P("seq", "ch")),
        check_vma=False,
    )
```

```python
import jax
import jax.numpy as jnp
from jax import lax
from jax.experimental import pallas as pl
from jax.experimental.pallas import tpu as pltpu
from jax.sharding import PartitionSpec as P

F32 = jnp.float32
BF16 = jnp.bfloat16
MESH = pl.DeviceIdType.MESH
FILT = 128
TOK = 1024
CH = 1024
OWN = 256
EB = 512
SPLIT = (0, 448)
QUART = (224, 288)

W_COPIES, A_COPIES, R_COPIES = 36, 13, 60
A_BASE = W_COPIES
R_BASE = A_BASE + A_COPIES
H_BASE = R_BASE + R_COPIES
F_BASE = H_BASE + 2
COPIES = F_BASE + 6


def kernel(
    q_hbm, k_hbm, v_hbm, f_ref, a_hbm, w_hbm,
    mx, kb, vb, gfo, gwo,
    qb, pe, ge, gt, afull, wfull, part,
    boxes, tbl, rback, rahead, gfr, g1, r1, g2, r2,
    ssem, rsem, lsem,
):
    s = lax.axis_index("seq")
    h = lax.axis_index("ch")
    y, z = s // 4, s % 4
    xx, core = h // 2, h % 2

    def at(c, by):
        return (c + by + 4) % 4

    def dev_y(by):
        return (at(y, by) * 4 + z, h)

    def dev_z(by):
        return (y * 4 + at(z, by), h)

    def dev_x(by):
        return (s, at(xx, by) * 2 + core)

    sibling = (s, xx * 2 + (1 - core))
    after = ((s + 1) % 16, h)
    before = ((s + 15) % 16, h)

    sent = []

    def send(src, dst, k, dev):
        c = pltpu.make_async_remote_copy(
            src_ref=src, dst_ref=dst, send_sem=ssem.at[k], recv_sem=rsem.at[k],
            device_id=dev, device_id_type=MESH,
        )
        c.start()
        sent.append(c)

    def arrived(dst, k):
        pltpu.make_async_remote_copy(
            src_ref=dst, dst_ref=dst, send_sem=ssem.at[k], recv_sem=rsem.at[k],
            device_id=sibling, device_id_type=MESH,
        ).wait_recv()

    def local(src, dst, k):
        c = pltpu.make_async_copy(src, dst, lsem.at[k])
        c.start()
        return c

    peers = [dev_y(1), dev_y(2), dev_y(3), dev_z(1), dev_z(2), dev_z(3), dev_x(1), dev_x(3), sibling, after, before]
    bar = pltpu.get_barrier_semaphore()
    for p in peers:
        pl.semaphore_signal(bar, inc=1, device_id=p, device_id_type=MESH)

    own_w = wfull.at[pl.ds(pl.multiple_of(s * OWN, OWN), OWN)]
    tail, rest = pl.ds(TOK - FILT, FILT), pl.ds(0, TOK - FILT)
    ld_tail = [local(k_hbm.at[tail], kb.at[tail], 0), local(v_hbm.at[tail], vb.at[tail], 1)]
    ld_rest = [local(k_hbm.at[rest], kb.at[rest], 2), local(v_hbm.at[rest], vb.at[rest], 3)]
    ld_q = local(q_hbm, qb, 4)
    ld_w = local(w_hbm, own_w, 5)
    ld_a = local(a_hbm, afull.at[h], 6)

    def product_rows(r):
        rows = pl.ds(r, 128)
        pe[pl.ds(r + FILT, 128)] = (kb[rows].astype(F32) * vb[rows].astype(F32)).astype(BF16)

    for c in ld_tail:
        c.wait()
    product_rows(TOK - FILT)
    pl.semaphore_wait(bar, len(peers))
    send(pe.at[pl.ds(TOK, FILT)], pe.at[pl.ds(0, FILT)], H_BASE, after)

    def wrows(yy, zz, start, size):
        return wfull.at[pl.ds(pl.multiple_of((yy * 4 + zz) * OWN + start, 64), size)]

    own_first = wrows(y, z, 0, 128)
    own_second = wrows(y, z, 128, 128)
    first_rows, second_rows = w_hbm.at[pl.ds(0, 128)], w_hbm.at[pl.ds(128, 128)]
    send(first_rows, own_first, 0, dev_z(1))
    send(first_rows, own_first, 1, dev_z(-1))
    send(first_rows, own_first, 2, dev_y(1))
    send(second_rows, own_second, 3, dev_y(-1))
    send(second_rows, own_second, 32, dev_z(1))
    send(second_rows, own_second, 33, dev_z(-1))
    send(second_rows, own_second, 34, dev_y(1))
    send(first_rows, own_first, 35, dev_y(-1))

    def ablk(bx, bc, half=None):
        r = afull.at[at(xx, bx) * 2 + bc]
        return r if half is None else r.at[pl.ds(half * 512, 512)]

    own_lo, own_hi = ablk(0, core, 0), ablk(0, core, 1)
    send(a_hbm.at[pl.ds(0, 512)], own_lo, A_BASE + 0, dev_x(1))
    send(a_hbm.at[pl.ds(512, 512)], own_hi, A_BASE + 1, dev_x(-1))
    send(a_hbm.at[pl.ds(512, 512)], own_hi, A_BASE + 2, dev_x(1))
    send(a_hbm.at[pl.ds(0, 512)], own_lo, A_BASE + 3, dev_x(-1))
    send(a_hbm, ablk(0, core), A_BASE + 4, sibling)

    def w1_z_minus():
        r = wrows(y, at(z, -1), 0, 128)
        arrived(r, 0)
        send(r, r, 4, dev_z(1))
        send(r, r, 8, dev_y(1))
        send(r, r, 9, dev_y(-1))

    def w1_z_plus():
        r = wrows(y, at(z, 1), 0, 128)
        arrived(r, 1)
        send(r, r, 10, dev_y(1))
        send(r, r, 11, dev_y(-1))

    def w1_z_plus_second():
        r = wrows(y, at(z, 1), 128, 128)
        arrived(r, 33)
        send(r, r, 5, dev_z(-1))

    def w1_y_minus():
        r = wrows(at(y, -1), z, 0, 128)
        arrived(r, 2)
        send(r, r, 6, dev_y(1))

    def w1_y_minus_second():
        r = wrows(at(y, -1), z, 128, 128)
        arrived(r, 34)
        send(r, r, 14, dev_z(1))
        send(r, r, 15, dev_z(-1))

    def w1_y_plus():
        r = wrows(at(y, 1), z, 128, 128)
        arrived(r, 3)
        send(r, r, 7, dev_y(-1))
        send(r, r, 16, dev_z(1))
        send(r, r, 17, dev_z(-1))

    def w2_z():
        r = wrows(y, at(z, 2), 0, 128)
        arrived(r, 4)
        send(r, r, 12, dev_y(1))
        send(r, r, 13, dev_y(-1))

    def w2_y():
        r = wrows(at(y, 2), z, 128, 128)
        arrived(r, 7)
        send(r, r, 18, dev_z(1))
        send(r, r, 19, dev_z(-1))

    def w3(i, piece):
        bz = (-1, 1, 2)[i]
        if piece == 0:
            r = wrows(at(y, -1), at(z, bz), 0, 128)
            arrived(r, 8 + 2 * i)
            r = wrows(at(y, -1), at(z, bz), 0, 64)
            send(r, r, 20 + 2 * i, dev_y(1))
        elif piece == 1:
            r = wrows(at(y, 1), at(z, bz), 0, 128)
            arrived(r, 9 + 2 * i)
            r = wrows(at(y, 1), at(z, bz), 64, 64)
            send(r, r, 21 + 2 * i, dev_y(-1))
        elif piece == 2:
            r = wrows(at(y, bz), at(z, -1), 128, 128)
            arrived(r, 14 + 2 * i)
            r = wrows(at(y, bz), at(z, -1), 128, 64)
            send(r, r, 26 + 2 * i, dev_z(1))
        else:
            r = wrows(at(y, bz), at(z, 1), 128, 128)
            arrived(r, 15 + 2 * i)
            r = wrows(at(y, bz), at(z, 1), 192, 64)
            send(r, r, 27 + 2 * i, dev_z(-1))

    def w_last():
        arrived(wrows(y, at(z, -1), 128, 128), 32)
        arrived(wrows(at(y, 1), z, 0, 128), 35)
        arrived(wrows(y, at(z, 2), 128, 128), 5)
        arrived(wrows(at(y, 2), z, 0, 128), 6)
        for i in range(3):
            bz = (-1, 1, 2)[i]
            arrived(wrows(at(y, 2), at(z, bz), 0, 64), 20 + 2 * i)
            arrived(wrows(at(y, 2), at(z, bz), 64, 64), 21 + 2 * i)
            arrived(wrows(at(y, bz), at(z, 2), 128, 64), 26 + 2 * i)
            arrived(wrows(at(y, bz), at(z, 2), 192, 64), 27 + 2 * i)

    def near(bx, half, k):
        r = ablk(bx, core, half)
        arrived(r, A_BASE + k)
        if k < 2:
            send(r, r, A_BASE + 5 + k, dev_x(-bx))
        send(r, r, A_BASE + 7 + (0, 1, 2, 3)[k], sibling)

    def far(half):
        r = ablk(2, core, half)
        arrived(r, A_BASE + 5 + half)
        send(r, r, A_BASE + 11 + half, sibling)

    def from_sibling(bx):
        if bx == 0:
            arrived(ablk(0, 1 - core), A_BASE + 4)
            return
        lo, hi = {-1: (7, 9), 1: (10, 8), 2: (11, 12)}[bx]
        arrived(ablk(bx, 1 - core, 0), A_BASE + lo)
        arrived(ablk(bx, 1 - core, 1), A_BASE + hi)

    def rs(hf, stage, i):
        along_z = (hf == 0) == (stage == 0)
        other = at(y if along_z else z, i)
        dev = dev_z if along_z else dev_y
        slot = hf * 5 + (i if stage == 0 else 4)
        base = R_BASE + slot * 6
        size = QUART[hf]

        def chunk(by, q):
            idx = other * 4 + at(z, by) if along_z else at(y, by) * 4 + other
            return part.at[idx, pl.ds(SPLIT[hf] + q * size, size)]

        def box(kind, q):
            return boxes.at[slot, kind * 2 + q, pl.ds(0, size)]

        def direct(q):
            by = (-1, 1)[q]
            send(chunk(by, 1 - q), box(1, q), base + 2 + q, dev(by))

        def start():
            send(chunk(2, 0), box(0, 0), base + 0, dev(-1))
            send(chunk(2, 1), box(0, 1), base + 1, dev(1))
            if stage == 0:
                direct(0)
                direct(1)

        def mid(q):
            by = (-1, 1)[q]
            arrived(box(0, q), base + q)
            c = chunk(by, q)
            c[...] = (c[...].astype(F32) + box(0, q)[...].astype(F32)).astype(BF16)
            send(c, box(2, q), base + 4 + q, dev(by))

        def fin():
            for kind in (1, 2):
                for q in (0, 1):
                    arrived(box(kind, q), base + 2 * kind + q)
            for q in (0, 1):
                c = chunk(0, q)
                total = c[...].astype(F32) + box(1, 1 - q)[...].astype(F32) + box(2, q)[...].astype(F32)
                if stage == 0:
                    c[...] = total.astype(BF16)
                else:
                    gwo[SPLIT[hf] + q * size : SPLIT[hf] + (q + 1) * size] = total.astype(BF16)

        return start, mid, fin, direct

    for c in ld_rest:
        c.wait()

    def product_loop(i, _):
        product_rows(pl.multiple_of(i * 128, 128))
        return 0

    lax.fori_loop(0, TOK // 128 - 1, product_loop, 0)

    tap = lax.broadcasted_iota(jnp.int32, (FILT, 256), 0)
    lane = lax.broadcasted_iota(jnp.int32, (FILT, 256), 1)
    f = f_ref[...]
    rback[...] = jnp.dot(f, (lane == FILT - tap).astype(F32).astype(BF16), preferred_element_type=F32)
    rahead[...] = jnp.dot(f, (lane == tap).astype(F32).astype(BF16), preferred_element_type=F32)
    group_of = (lane % 128) // 16

    def lanes_of(L):
        return pl.ds(pl.multiple_of(L * 128, 128), 128)

    def make_table(rows_ref, L):
        rows = rows_ref[pl.ds(pl.multiple_of(L * 8, 8), 8), :]
        for g in range(8):
            wide = jnp.broadcast_to(rows[g : g + 1, :], (FILT, 256))
            tbl[g * FILT : (g + 1) * FILT, :] = pltpu.roll(wide, 0, 1, stride=1, stride_axis=0).astype(BF16)

    def windows(ref, p, lanes):
        return jnp.concatenate([ref[pl.ds(p * 256, 256), lanes], ref[pl.ds(p * 256 + 128, 256), lanes]], axis=1)

    def filtered(ref, p, lanes):
        res = jnp.dot(tbl[...], windows(ref, p, lanes), preferred_element_type=F32)
        out = res[0:FILT]
        for g in range(1, 8):
            out = jnp.where(group_of == g, res[g * FILT : (g + 1) * FILT], out)
        return jnp.concatenate([out[:, :128], out[:, 128:]], axis=0)

    def conv_mixed(L, _):
        lanes = lanes_of(L)
        make_table(rback, L)
        for p in range(4):
            m = filtered(pe, p, lanes)
            rows = pl.ds(p * 256, 256)
            mx[rows, lanes] = m.astype(BF16)
            gated = (qb[rows, lanes].astype(F32) * m).astype(BF16)
            gt[lanes, rows] = gated.T
        return 0

    def prior_product():
        arrived(pe.at[pl.ds(0, FILT)], H_BASE)

        @pl.when(s == 0)
        def _():
            pe[pl.ds(0, FILT)] = jnp.zeros((FILT, CH), BF16)

        ld_q.wait()

    def weight_grad(bx, bc):
        blk = at(xx, bx) * 2 + bc

        def one(u, _):
            cols = pl.ds(pl.multiple_of(u * 256, 256), 256)
            r = jnp.dot(gt[...], afull[blk, :, cols], preferred_element_type=F32)
            part[blk * 2 + u] = r.astype(BF16)
            return 0

        lax.fori_loop(0, 2, one, 0)

    def rs_x(bx):
        return rs(0, 0, (xx + bx - y + 8) % 4)

    start, mid, fin, direct = 0, 1, 2, 3

    def gated_grad(n, _):
        cols = pl.ds(pl.multiple_of(n * 256, 256), 256)
        acc = jnp.dot(afull[0], wfull[pl.ds(0, EB), cols], preferred_element_type=F32)
        for b in range(1, 8):
            acc = acc + jnp.dot(afull[b], wfull[pl.ds(b * EB, EB), cols], preferred_element_type=F32)
        gg = acc.astype(BF16).astype(F32)
        ge[pl.ds(0, TOK), cols] = (gg * qb[:, cols].astype(F32)).astype(BF16)
        mx[:, cols] = (gg * mx[:, cols].astype(F32)).astype(BF16)
        return 0

    def send_mixed_halo():
        send(ge.at[pl.ds(0, FILT)], ge.at[pl.ds(TOK, FILT)], H_BASE + 1, before)

    flip = (lax.broadcasted_iota(jnp.int32, (FILT, FILT), 0) + lax.broadcasted_iota(jnp.int32, (FILT, FILT), 1) == FILT - 1)
    flip = flip.astype(F32).astype(BF16)

    def lag_products(L, _):
        lanes = lanes_of(L)
        acc = None
        for p in range(4):
            own = jnp.concatenate([ge[pl.ds(p * 256, 128), lanes], ge[pl.ds(p * 256 + 128, 128), lanes]], axis=1)
            own = jnp.dot(flip, own, preferred_element_type=F32)
            lhs = jnp.concatenate([jnp.where(group_of == g, own, 0.0).astype(BF16) for g in range(8)], axis=0)
            d = lax.dot_general(lhs, windows(pe, p, lanes), (((1,), (1,)), ((), ())), preferred_element_type=F32)
            acc = d if acc is None else acc + d
        sums = []
        for g in range(8):
            skew = pltpu.roll(acc[g * FILT : (g + 1) * FILT], 0, 1, stride=1, stride_axis=0)
            sums.append(jnp.sum(skew, axis=0, keepdims=True))
        gfr[pl.ds(pl.multiple_of(L * 8, 8), 8), :] = jnp.concatenate(sums, axis=0)
        return 0

    def send_taps_z():
        pick = (lane == 255 - tap).astype(F32).astype(BF16)
        hi = gfr[...].astype(BF16)
        lo = (gfr[...] - hi.astype(F32)).astype(BF16)
        nt = (((1,), (1,)), ((), ()))
        taps = lax.dot_general(pick, hi, nt, preferred_element_type=F32)
        taps = taps + lax.dot_general(pick, lo, nt, preferred_element_type=F32)
        for i in range(16):
            g1[i % 4, i // 4] = taps[i * 8 : (i + 1) * 8]
        for d in (1, 2, 3):
            send(g1.at[at(z, d)], r1.at[d - 1], F_BASE + d - 1, dev_z(d))

    def send_taps_y():
        for d in (1, 2, 3):
            arrived(r1.at[d - 1], F_BASE + d - 1)
        g2[...] = g1[z] + r1[0] + r1[1] + r1[2]
        for d in (1, 2, 3):
            send(g2.at[at(y, d)], r2.at[d - 1], F_BASE + 2 + d, dev_y(d))

    def sum_taps():
        for d in (1, 2, 3):
            arrived(r2.at[d - 1], F_BASE + 2 + d)
        gfo[...] = g2[y] + r2[0] + r2[1] + r2[2]

    def later_mixed():
        arrived(ge.at[pl.ds(TOK, FILT)], H_BASE + 1)

        @pl.when(s == 15)
        def _():
            ge[pl.ds(TOK, FILT)] = jnp.zeros((FILT, CH), BF16)

    def conv_grad(L, _):
        lanes = lanes_of(L)
        make_table(rahead, L)
        for p in range(4):
            m = filtered(ge, p, lanes)
            rows = pl.ds(p * 256, 256)
            keys, values = kb[rows, lanes].astype(F32), vb[rows, lanes].astype(F32)
            kb[rows, lanes] = (m * values).astype(BF16)
            vb[rows, lanes] = (m * keys).astype(BF16)
        return 0

    ld_w.wait()
    w1_y_plus()
    w1_z_plus()
    prior_product()
    lax.fori_loop(0, 2, conv_mixed, 0)
    w1_z_minus()
    lax.fori_loop(2, 3, conv_mixed, 0)
    near(1, 1, 1)
    w1_y_minus_second()
    near(-1, 0, 0)
    lax.fori_loop(3, 6, conv_mixed, 0)
    w1_z_plus_second()
    lax.fori_loop(6, 8, conv_mixed, 0)
    w1_y_minus()
    ld_a.wait()
    weight_grad(0, core)
    near(1, 0, 3)
    w2_y()
    w3(1, 2)
    w3(1, 1)
    w3(1, 0)
    weight_grad(1, core)
    w3(1, 3)
    from_sibling(0)
    weight_grad(0, 1 - core)
    near(-1, 1, 2)
    w3(0, 3)
    w2_z()
    w3(0, 0)
    from_sibling(1)
    weight_grad(1, 1 - core)
    w3(0, 1)
    weight_grad(-1, core)
    far(1)
    from_sibling(-1)
    weight_grad(-1, 1 - core)
    far(0)
    w3(0, 2)
    w3(2, 3)
    weight_grad(2, core)
    w3(2, 0)
    w3(2, 1)
    from_sibling(2)
    weight_grad(2, 1 - core)
    w3(2, 2)
    rs_x(1)[start]()
    rs(1, 0, 1)[start]()
    rs_x(-1)[start]()
    rs(1, 0, 0)[start]()
    rs(1, 0, 1)[mid](0)
    rs_x(0)[start]()
    w_last()
    lax.fori_loop(0, 1, gated_grad, 0)
    rs_x(-1)[mid](0)
    rs(1, 0, 2)[start]()
    lax.fori_loop(1, 3, gated_grad, 0)
    rs_x(2)[start]()
    rs(1, 0, 1)[mid](1)
    lax.fori_loop(3, 4, gated_grad, 0)
    send_mixed_halo()
    rs(1, 0, 3)[start]()
    gfr[...] = jnp.zeros((128, 256), F32)
    lax.fori_loop(0, 2, lag_products, 0)
    rs_x(0)[mid](0)
    lax.fori_loop(2, 3, lag_products, 0)
    rs(1, 0, 2)[mid](0)
    lax.fori_loop(3, 4, lag_products, 0)
    rs(1, 0, 2)[mid](1)
    rs_x(1)[mid](1)
    rs_x(-1)[mid](1)
    rs_x(0)[mid](1)
    lax.fori_loop(4, 5, lag_products, 0)
    rs_x(2)[mid](1)
    rs_x(1)[mid](0)
    rs_x(2)[mid](0)
    lax.fori_loop(5, 6, lag_products, 0)
    rs(1, 0, 3)[mid](0)
    lax.fori_loop(6, 8, lag_products, 0)
    later_mixed()
    lax.fori_loop(0, 1, conv_grad, 0)
    rs(1, 0, 3)[mid](1)
    lax.fori_loop(1, 2, conv_grad, 0)
    rs(1, 0, 0)[mid](1)
    rs(1, 0, 0)[mid](0)
    send_taps_z()
    lax.fori_loop(2, 3, conv_grad, 0)
    rs(1, 0, 2)[fin]()
    rs(1, 1, 0)[start]()
    lax.fori_loop(3, 5, conv_grad, 0)
    rs(1, 0, 1)[fin]()
    rs(1, 1, 0)[direct](1)
    rs(0, 0, 2)[fin]()
    rs(0, 1, 0)[start]()
    rs(1, 0, 3)[fin]()
    rs(1, 1, 0)[direct](0)
    rs(0, 0, 3)[fin]()
    rs(0, 0, 1)[fin]()
    send_taps_y()
    rs(0, 1, 0)[direct](0)
    rs(0, 1, 0)[direct](1)
    rs(1, 1, 0)[mid](0)
    lax.fori_loop(5, 6, conv_grad, 0)
    rs(0, 0, 0)[fin]()
    rs(1, 1, 0)[mid](1)
    rs(0, 1, 0)[mid](0)
    rs(0, 1, 0)[mid](1)
    rs(1, 0, 0)[fin]()
    lax.fori_loop(6, 7, conv_grad, 0)
    sum_taps()
    lax.fori_loop(7, 8, conv_grad, 0)
    rs(1, 1, 0)[fin]()
    rs(0, 1, 0)[fin]()
    for c in sent:
        c.wait_send()


def store(gq, gk, gv, gf, gw, gq_out, gk_out, gv_out, gf_out, gw_out, sem):
    copies = [
        pltpu.make_async_copy(src.at[pl.ds(r * 256, 256)], dst.at[pl.ds(r * 256, 256)], sem.at[i, r])
        for r in range(4)
        for i, (src, dst) in enumerate(((gq, gq_out), (gk, gk_out), (gv, gv_out)))
    ]
    for c in copies:
        c.start()
    gw_out[...] = gw[...].T
    gf_out[...] = gf[:, :64]
    for c in copies:
        c.wait()


def shards(queries, keys, values, filters, grad_out, out_weight):
    hbm = pl.BlockSpec(memory_space=pl.ANY)
    vm = pltpu.VMEM
    out = pl.pallas_call(
        kernel,
        out_shape=(
            vm((TOK, CH), BF16),
            vm((TOK, CH), BF16),
            vm((TOK, CH), BF16),
            vm((8, 128), F32),
            vm((CH, OWN), BF16),
        ),
        in_specs=[hbm, hbm, hbm, pl.BlockSpec(memory_space=pltpu.VMEM), hbm, hbm],
        out_specs=(pl.BlockSpec(memory_space=pltpu.VMEM),) * 5,
        scratch_shapes=[
            vm((TOK, CH), BF16),
            vm((TOK + FILT, CH), BF16),
            vm((TOK + FILT, CH), BF16),
            vm((CH, TOK), BF16),
            vm((8, TOK, EB), BF16),
            vm((4096, CH), BF16),
            vm((16, CH, OWN), BF16),
            vm((10, 6, max(QUART), OWN), BF16),
            vm((1024, 256), BF16),
            vm((64, 256), F32),
            vm((64, 256), F32),
            vm((128, 256), F32),
            vm((4, 4, 8, 128), F32),
            vm((3, 4, 8, 128), F32),
            vm((4, 8, 128), F32),
            vm((3, 8, 128), F32),
            pltpu.SemaphoreType.DMA((COPIES,)),
            pltpu.SemaphoreType.DMA((COPIES,)),
            pltpu.SemaphoreType.DMA((7,)),
        ],
        compiler_params=pltpu.CompilerParams(
            collective_id=0, has_side_effects=True, vmem_limit_bytes=53 * 1024 * 1024
        ),
        name="hyena_bwd",
    )(queries, keys, values, filters, grad_out, out_weight)
    gq, gk, gv, gf, gw = pl.pallas_call(
        store,
        out_shape=(
            jax.ShapeDtypeStruct((TOK, CH), BF16),
            jax.ShapeDtypeStruct((TOK, CH), BF16),
            jax.ShapeDtypeStruct((TOK, CH), BF16),
            jax.ShapeDtypeStruct((8, 64), F32),
            jax.ShapeDtypeStruct((OWN, CH), BF16),
        ),
        in_specs=[hbm] * 3 + [pl.BlockSpec(memory_space=vm)] * 2,
        out_specs=(hbm,) * 3 + (pl.BlockSpec(memory_space=vm),) * 2,
        scratch_shapes=[pltpu.SemaphoreType.DMA((3, 4))],
        compiler_params=pltpu.CompilerParams(vmem_limit_bytes=4 * 1024 * 1024),
        name="store",
    )(*out)
    return gq, gk, gv, gf.T, gw


def solution(mesh):
    return jax.shard_map(
        shards,
        mesh=mesh,
        in_specs=(
            P("seq", "ch"),
            P("seq", "ch"),
            P("seq", "ch"),
            P("ch", None),
            P("seq", "ch"),
            P("seq", "ch"),
        ),
        out_specs=(P("seq", "ch"), P("seq", "ch"), P("seq", "ch"), P("ch", "seq"), P("seq", "ch")),
        check_vma=False,
    )
```

```python
import jax
import jax.numpy as jnp
from jax import lax
from jax.experimental import pallas as pl
from jax.experimental.pallas import tpu as pltpu
from jax.sharding import PartitionSpec as P

F32 = jnp.float32
BF16 = jnp.bfloat16
MESH = pl.DeviceIdType.MESH
FILT = 128
TOK = 1024
CH = 1024
OWN = 256
EB = 512
SPLIT = (0, 448)
QUART = (224, 288)

W_COPIES, A_COPIES, R_COPIES = 36, 13, 60
A_BASE = W_COPIES
R_BASE = A_BASE + A_COPIES
H_BASE = R_BASE + R_COPIES
F_BASE = H_BASE + 2
COPIES = F_BASE + 6


def kernel(
    q_hbm, k_hbm, v_hbm, f_ref, a_hbm, w_hbm,
    mx, kb, vb, gfo, gwo,
    qb, pe, ge, gt, afull, wfull, part,
    boxes, tbl, rback, rahead, gfr, g1, r1, g2, r2,
    ssem, rsem, lsem,
):
    s = lax.axis_index("seq")
    h = lax.axis_index("ch")
    y, z = s // 4, s % 4
    xx, core = h // 2, h % 2

    def at(c, by):
        return (c + by + 4) % 4

    def dev_y(by):
        return (at(y, by) * 4 + z, h)

    def dev_z(by):
        return (y * 4 + at(z, by), h)

    def dev_x(by):
        return (s, at(xx, by) * 2 + core)

    sibling = (s, xx * 2 + (1 - core))
    after = ((s + 1) % 16, h)
    before = ((s + 15) % 16, h)

    sent = []

    def send(src, dst, k, dev):
        c = pltpu.make_async_remote_copy(
            src_ref=src, dst_ref=dst, send_sem=ssem.at[k], recv_sem=rsem.at[k],
            device_id=dev, device_id_type=MESH,
        )
        c.start()
        sent.append(c)

    def arrived(dst, k):
        pltpu.make_async_remote_copy(
            src_ref=dst, dst_ref=dst, send_sem=ssem.at[k], recv_sem=rsem.at[k],
            device_id=sibling, device_id_type=MESH,
        ).wait_recv()

    def local(src, dst, k):
        c = pltpu.make_async_copy(src, dst, lsem.at[k])
        c.start()
        return c

    peers = [dev_y(1), dev_y(2), dev_y(3), dev_z(1), dev_z(2), dev_z(3), dev_x(1), dev_x(3), sibling, after, before]
    bar = pltpu.get_barrier_semaphore()
    for p in peers:
        pl.semaphore_signal(bar, inc=1, device_id=p, device_id_type=MESH)

    own_w = wfull.at[pl.ds(pl.multiple_of(s * OWN, OWN), OWN)]
    tail, rest = pl.ds(TOK - FILT, FILT), pl.ds(0, TOK - FILT)
    ld_tail = [local(k_hbm.at[tail], kb.at[tail], 0), local(v_hbm.at[tail], vb.at[tail], 1)]
    ld_rest = [local(k_hbm.at[rest], kb.at[rest], 2), local(v_hbm.at[rest], vb.at[rest], 3)]
    ld_q = local(q_hbm, qb, 4)
    ld_w = local(w_hbm, own_w, 5)
    ld_a = local(a_hbm, afull.at[h], 6)

    def product_rows(r):
        rows = pl.ds(r, 128)
        pe[pl.ds(r + FILT, 128)] = (kb[rows].astype(F32) * vb[rows].astype(F32)).astype(BF16)

    pl.semaphore_wait(bar, len(peers))

    def wrows(yy, zz, start, size):
        return wfull.at[pl.ds(pl.multiple_of((yy * 4 + zz) * OWN + start, 64), size)]

    own_first = wrows(y, z, 0, 128)
    own_second = wrows(y, z, 128, 128)
    first_rows, second_rows = w_hbm.at[pl.ds(0, 128)], w_hbm.at[pl.ds(128, 128)]
    send(first_rows, own_first, 0, dev_z(1))
    send(first_rows, own_first, 1, dev_z(-1))
    send(first_rows, own_first, 2, dev_y(1))
    send(second_rows, own_second, 3, dev_y(-1))
    send(second_rows, own_second, 33, dev_z(-1))
    send(second_rows, own_second, 34, dev_y(1))
    send(first_rows, own_first, 35, dev_y(-1))

    def ablk(bx, bc, half=None):
        r = afull.at[at(xx, bx) * 2 + bc]
        return r if half is None else r.at[pl.ds(half * 512, 512)]

    own_lo, own_hi = ablk(0, core, 0), ablk(0, core, 1)
    send(a_hbm.at[pl.ds(0, 512)], own_lo, A_BASE + 0, dev_x(1))
    send(a_hbm.at[pl.ds(512, 512)], own_hi, A_BASE + 1, dev_x(-1))
    send(a_hbm.at[pl.ds(512, 512)], own_hi, A_BASE + 2, dev_x(1))
    send(a_hbm.at[pl.ds(0, 512)], own_lo, A_BASE + 3, dev_x(-1))
    send(a_hbm, ablk(0, core), A_BASE + 4, sibling)

    def w1_z_minus():
        r = wrows(y, at(z, -1), 0, 128)
        arrived(r, 0)
        send(r, r, 4, dev_z(1))
        send(r, r, 8, dev_y(1))
        send(r, r, 9, dev_y(-1))

    def w1_z_plus():
        r = wrows(y, at(z, 1), 0, 128)
        arrived(r, 1)
        send(r, r, 10, dev_y(1))
        send(r, r, 11, dev_y(-1))

    def w1_z_plus_second():
        r = wrows(y, at(z, 1), 128, 128)
        arrived(r, 33)
        send(r, r, 5, dev_z(-1))

    def w1_y_minus():
        r = wrows(at(y, -1), z, 0, 128)
        arrived(r, 2)
        send(r, r, 6, dev_y(1))

    def w1_y_minus_second():
        r = wrows(at(y, -1), z, 128, 128)
        arrived(r, 34)
        send(r, r, 14, dev_z(1))
        send(r, r, 15, dev_z(-1))

    def w1_y_plus():
        r = wrows(at(y, 1), z, 128, 128)
        arrived(r, 3)
        send(r, r, 7, dev_y(-1))
        send(r, r, 16, dev_z(1))
        send(r, r, 17, dev_z(-1))

    def w2_z():
        r = wrows(y, at(z, 2), 0, 128)
        arrived(r, 4)
        send(r, r, 12, dev_y(1))
        send(r, r, 13, dev_y(-1))

    def w2_y():
        r = wrows(at(y, 2), z, 128, 128)
        arrived(r, 7)
        send(r, r, 18, dev_z(1))
        send(r, r, 19, dev_z(-1))

    def w3(i, piece):
        bz = (-1, 1, 2)[i]
        if piece == 0:
            r = wrows(at(y, -1), at(z, bz), 0, 128)
            arrived(r, 8 + 2 * i)
            r = wrows(at(y, -1), at(z, bz), 0, 64)
            send(r, r, 20 + 2 * i, dev_y(1))
        elif piece == 1:
            r = wrows(at(y, 1), at(z, bz), 0, 128)
            arrived(r, 9 + 2 * i)
            r = wrows(at(y, 1), at(z, bz), 64, 64)
            send(r, r, 21 + 2 * i, dev_y(-1))
        elif piece == 2:
            r = wrows(at(y, bz), at(z, -1), 128, 128)
            arrived(r, 14 + 2 * i)
            r = wrows(at(y, bz), at(z, -1), 128, 64)
            send(r, r, 26 + 2 * i, dev_z(1))
        else:
            r = wrows(at(y, bz), at(z, 1), 128, 128)
            arrived(r, 15 + 2 * i)
            r = wrows(at(y, bz), at(z, 1), 192, 64)
            send(r, r, 27 + 2 * i, dev_z(-1))

    def w_last():
        arrived(wrows(y, at(z, -1), 128, 128), 32)
        arrived(wrows(at(y, 1), z, 0, 128), 35)
        arrived(wrows(y, at(z, 2), 128, 128), 5)
        arrived(wrows(at(y, 2), z, 0, 128), 6)
        for i in range(3):
            bz = (-1, 1, 2)[i]
            arrived(wrows(at(y, 2), at(z, bz), 0, 64), 20 + 2 * i)
            arrived(wrows(at(y, 2), at(z, bz), 64, 64), 21 + 2 * i)
            arrived(wrows(at(y, bz), at(z, 2), 128, 64), 26 + 2 * i)
            arrived(wrows(at(y, bz), at(z, 2), 192, 64), 27 + 2 * i)

    def near(bx, half, k):
        r = ablk(bx, core, half)
        arrived(r, A_BASE + k)
        if k < 2:
            send(r, r, A_BASE + 5 + k, dev_x(-bx))
        send(r, r, A_BASE + 7 + (0, 1, 2, 3)[k], sibling)

    def far(half):
        r = ablk(2, core, half)
        arrived(r, A_BASE + 5 + half)
        send(r, r, A_BASE + 11 + half, sibling)

    def from_sibling(bx):
        if bx == 0:
            arrived(ablk(0, 1 - core), A_BASE + 4)
            return
        lo, hi = {-1: (7, 9), 1: (10, 8), 2: (11, 12)}[bx]
        arrived(ablk(bx, 1 - core, 0), A_BASE + lo)
        arrived(ablk(bx, 1 - core, 1), A_BASE + hi)

    def rs(hf, stage, i):
        along_z = (hf == 0) == (stage == 0)
        other = at(y if along_z else z, i)
        dev = dev_z if along_z else dev_y
        slot = hf * 5 + (i if stage == 0 else 4)
        base = R_BASE + slot * 6
        size = QUART[hf]

        def chunk(by, q):
            idx = other * 4 + at(z, by) if along_z else at(y, by) * 4 + other
            return part.at[idx, pl.ds(SPLIT[hf] + q * size, size)]

        def box(kind, q):
            return boxes.at[slot, kind * 2 + q, pl.ds(0, size)]

        def direct(q):
            by = (-1, 1)[q]
            send(chunk(by, 1 - q), box(1, q), base + 2 + q, dev(by))

        def start():
            send(chunk(2, 0), box(0, 0), base + 0, dev(-1))
            send(chunk(2, 1), box(0, 1), base + 1, dev(1))
            if stage == 0:
                direct(0)
                direct(1)

        def mid(q):
            by = (-1, 1)[q]
            arrived(box(0, q), base + q)
            c = chunk(by, q)
            c[...] = (c[...].astype(F32) + box(0, q)[...].astype(F32)).astype(BF16)
            send(c, box(2, q), base + 4 + q, dev(by))

        def fin():
            for kind in (1, 2):
                for q in (0, 1):
                    arrived(box(kind, q), base + 2 * kind + q)
            for q in (0, 1):
                c = chunk(0, q)
                total = c[...].astype(F32) + box(1, 1 - q)[...].astype(F32) + box(2, q)[...].astype(F32)
                if stage == 0:
                    c[...] = total.astype(BF16)
                else:
                    gwo[SPLIT[hf] + q * size : SPLIT[hf] + (q + 1) * size] = total.astype(BF16)

        return start, mid, fin, direct

    for c in ld_tail:
        c.wait()
    product_rows(TOK - FILT)
    send(pe.at[pl.ds(TOK, FILT)], pe.at[pl.ds(0, FILT)], H_BASE, after)
    send(second_rows, own_second, 32, dev_z(1))
    for c in ld_rest:
        c.wait()

    def product_loop(i, _):
        product_rows(pl.multiple_of(i * 128, 128))
        return 0

    lax.fori_loop(0, TOK // 128 - 1, product_loop, 0)

    tap = lax.broadcasted_iota(jnp.int32, (FILT, 256), 0)
    lane = lax.broadcasted_iota(jnp.int32, (FILT, 256), 1)
    f = f_ref[...]
    rback[...] = jnp.dot(f, (lane == FILT - tap).astype(F32).astype(BF16), preferred_element_type=F32)
    rahead[...] = jnp.dot(f, (lane == tap).astype(F32).astype(BF16), preferred_element_type=F32)
    group_of = (lane % 128) // 16

    def lanes_of(L):
        return pl.ds(pl.multiple_of(L * 128, 128), 128)

    def make_table(rows_ref, L):
        rows = rows_ref[pl.ds(pl.multiple_of(L * 8, 8), 8), :]
        for g in range(8):
            wide = jnp.broadcast_to(rows[g : g + 1, :], (FILT, 256))
            tbl[g * FILT : (g + 1) * FILT, :] = pltpu.roll(wide, 0, 1, stride=1, stride_axis=0).astype(BF16)

    def windows(ref, p, lanes):
        return jnp.concatenate([ref[pl.ds(p * 256, 256), lanes], ref[pl.ds(p * 256 + 128, 256), lanes]], axis=1)

    def filtered(ref, p, lanes):
        res = jnp.dot(tbl[...], windows(ref, p, lanes), preferred_element_type=F32)
        out = res[0:FILT]
        for g in range(1, 8):
            out = jnp.where(group_of == g, res[g * FILT : (g + 1) * FILT], out)
        return jnp.concatenate([out[:, :128], out[:, 128:]], axis=0)

    def conv_mixed(L, _):
        lanes = lanes_of(L)
        make_table(rback, L)
        for p in range(4):
            m = filtered(pe, p, lanes)
            rows = pl.ds(p * 256, 256)
            mx[rows, lanes] = m.astype(BF16)
            gated = (qb[rows, lanes].astype(F32) * m).astype(BF16)
            gt[lanes, rows] = gated.T
        return 0

    def prior_product():
        arrived(pe.at[pl.ds(0, FILT)], H_BASE)

        @pl.when(s == 0)
        def _():
            pe[pl.ds(0, FILT)] = jnp.zeros((FILT, CH), BF16)

        ld_q.wait()

    def weight_grad(bx, bc):
        blk = at(xx, bx) * 2 + bc

        def one(u, _):
            cols = pl.ds(pl.multiple_of(u * 256, 256), 256)
            r = jnp.dot(gt[...], afull[blk, :, cols], preferred_element_type=F32)
            part[blk * 2 + u] = r.astype(BF16)
            return 0

        lax.fori_loop(0, 2, one, 0)

    def rs_x(bx):
        return rs(0, 0, (xx + bx - y + 8) % 4)

    start, mid, fin, direct = 0, 1, 2, 3

    def gated_grad(n, _):
        cols = pl.ds(pl.multiple_of(n * 256, 256), 256)
        acc = jnp.dot(afull[0], wfull[pl.ds(0, EB), cols], preferred_element_type=F32)
        for b in range(1, 8):
            acc = acc + jnp.dot(afull[b], wfull[pl.ds(b * EB, EB), cols], preferred_element_type=F32)
        gg = acc.astype(BF16).astype(F32)
        ge[pl.ds(0, TOK), cols] = (gg * qb[:, cols].astype(F32)).astype(BF16)
        mx[:, cols] = (gg * mx[:, cols].astype(F32)).astype(BF16)
        return 0

    def send_mixed_halo():
        send(ge.at[pl.ds(0, FILT)], ge.at[pl.ds(TOK, FILT)], H_BASE + 1, before)

    flip = (lax.broadcasted_iota(jnp.int32, (FILT, FILT), 0) + lax.broadcasted_iota(jnp.int32, (FILT, FILT), 1) == FILT - 1)
    flip = flip.astype(F32).astype(BF16)

    def lag_products(L, _):
        lanes = lanes_of(L)
        acc = None
        for p in range(4):
            own = jnp.concatenate([ge[pl.ds(p * 256, 128), lanes], ge[pl.ds(p * 256 + 128, 128), lanes]], axis=1)
            own = jnp.dot(flip, own, preferred_element_type=F32)
            lhs = jnp.concatenate([jnp.where(group_of == g, own, 0.0).astype(BF16) for g in range(8)], axis=0)
            d = lax.dot_general(lhs, windows(pe, p, lanes), (((1,), (1,)), ((), ())), preferred_element_type=F32)
            acc = d if acc is None else acc + d
        sums = []
        for g in range(8):
            skew = pltpu.roll(acc[g * FILT : (g + 1) * FILT], 0, 1, stride=1, stride_axis=0)
            sums.append(jnp.sum(skew, axis=0, keepdims=True))
        gfr[pl.ds(pl.multiple_of(L * 8, 8), 8), :] = jnp.concatenate(sums, axis=0)
        return 0

    def send_taps_z():
        pick = (lane == 255 - tap).astype(F32).astype(BF16)
        hi = gfr[...].astype(BF16)
        lo = (gfr[...] - hi.astype(F32)).astype(BF16)
        nt = (((1,), (1,)), ((), ()))
        taps = lax.dot_general(pick, hi, nt, preferred_element_type=F32)
        taps = taps + lax.dot_general(pick, lo, nt, preferred_element_type=F32)
        for i in range(16):
            g1[i % 4, i // 4] = taps[i * 8 : (i + 1) * 8]
        for d in (1, 2, 3):
            send(g1.at[at(z, d)], r1.at[d - 1], F_BASE + d - 1, dev_z(d))

    def send_taps_y():
        for d in (1, 2, 3):
            arrived(r1.at[d - 1], F_BASE + d - 1)
        g2[...] = g1[z] + r1[0] + r1[1] + r1[2]
        for d in (1, 2, 3):
            send(g2.at[at(y, d)], r2.at[d - 1], F_BASE + 2 + d, dev_y(d))

    def sum_taps():
        for d in (1, 2, 3):
            arrived(r2.at[d - 1], F_BASE + 2 + d)
        gfo[...] = g2[y] + r2[0] + r2[1] + r2[2]

    def later_mixed():
        arrived(ge.at[pl.ds(TOK, FILT)], H_BASE + 1)

        @pl.when(s == 15)
        def _():
            ge[pl.ds(TOK, FILT)] = jnp.zeros((FILT, CH), BF16)

    def conv_grad(L, _):
        lanes = lanes_of(L)
        make_table(rahead, L)
        for p in range(4):
            m = filtered(ge, p, lanes)
            rows = pl.ds(p * 256, 256)
            keys, values = kb[rows, lanes].astype(F32), vb[rows, lanes].astype(F32)
            kb[rows, lanes] = (m * values).astype(BF16)
            vb[rows, lanes] = (m * keys).astype(BF16)
        return 0

    ld_w.wait()
    w1_z_minus()
    w1_y_plus()
    w1_z_plus()
    w1_y_minus_second()
    near(-1, 0, 0)
    prior_product()
    lax.fori_loop(0, 2, conv_mixed, 0)
    near(1, 1, 1)
    lax.fori_loop(2, 5, conv_mixed, 0)
    w3(1, 3)
    lax.fori_loop(5, 6, conv_mixed, 0)
    w1_y_minus()
    lax.fori_loop(6, 8, conv_mixed, 0)
    w2_y()
    w1_z_plus_second()
    w2_z()
    w3(0, 1)
    near(-1, 1, 2)
    ld_a.wait()
    from_sibling(0)
    weight_grad(0, 1 - core)
    weight_grad(-1, core)
    weight_grad(0, core)
    from_sibling(-1)
    weight_grad(-1, 1 - core)
    w3(1, 0)
    w3(1, 1)
    near(1, 0, 3)
    w3(2, 3)
    w3(1, 2)
    weight_grad(1, core)
    far(1)
    w3(0, 3)
    far(0)
    w3(2, 0)
    w3(0, 2)
    weight_grad(2, core)
    from_sibling(1)
    weight_grad(1, 1 - core)
    w3(0, 0)
    w3(2, 1)
    w3(2, 2)
    rs_x(-1)[start]()
    from_sibling(2)
    weight_grad(2, 1 - core)
    rs(1, 0, 3)[start]()
    rs_x(2)[start]()
    rs(1, 0, 2)[start]()
    rs_x(0)[start]()
    rs_x(1)[start]()
    w_last()
    rs(1, 0, 1)[start]()
    lax.fori_loop(0, 1, gated_grad, 0)
    rs(1, 0, 3)[mid](1)
    lax.fori_loop(1, 4, gated_grad, 0)
    gfr[...] = jnp.zeros((128, 256), F32)
    lax.fori_loop(0, 2, lag_products, 0)
    rs(1, 0, 2)[mid](0)
    send_mixed_halo()
    lax.fori_loop(2, 3, lag_products, 0)
    rs(1, 0, 2)[mid](1)
    lax.fori_loop(3, 4, lag_products, 0)
    rs_x(0)[mid](0)
    rs(1, 0, 1)[mid](0)
    rs_x(-1)[mid](0)
    rs_x(2)[mid](1)
    rs_x(-1)[mid](1)
    rs(1, 0, 1)[mid](1)
    lax.fori_loop(4, 6, lag_products, 0)
    rs(1, 0, 3)[mid](0)
    lax.fori_loop(6, 8, lag_products, 0)
    rs(1, 0, 0)[start]()
    rs_x(2)[mid](0)
    later_mixed()
    lax.fori_loop(0, 1, conv_grad, 0)
    rs_x(1)[mid](1)
    rs_x(0)[mid](1)
    rs(1, 0, 2)[fin]()
    rs_x(1)[mid](0)
    lax.fori_loop(1, 2, conv_grad, 0)
    send_taps_z()
    lax.fori_loop(2, 3, conv_grad, 0)
    rs(1, 0, 1)[fin]()
    lax.fori_loop(3, 4, conv_grad, 0)
    rs(1, 0, 0)[mid](1)
    rs(1, 1, 0)[start]()
    rs(1, 0, 0)[mid](0)
    lax.fori_loop(4, 5, conv_grad, 0)
    rs(1, 1, 0)[direct](1)
    rs(1, 0, 3)[fin]()
    rs(0, 0, 2)[fin]()
    rs(0, 1, 0)[start]()
    rs(1, 1, 0)[direct](0)
    rs(0, 0, 3)[fin]()
    rs(0, 0, 1)[fin]()
    lax.fori_loop(5, 6, conv_grad, 0)
    send_taps_y()
    rs(0, 1, 0)[direct](1)
    rs(0, 1, 0)[direct](0)
    rs(1, 1, 0)[mid](0)
    rs(1, 1, 0)[mid](1)
    rs(0, 1, 0)[mid](0)
    rs(0, 1, 0)[mid](1)
    lax.fori_loop(6, 7, conv_grad, 0)
    rs(0, 0, 0)[fin]()
    lax.fori_loop(7, 8, conv_grad, 0)
    rs(1, 0, 0)[fin]()
    sum_taps()
    rs(1, 1, 0)[fin]()
    rs(0, 1, 0)[fin]()
    for c in sent:
        c.wait_send()


def store(gq, gk, gv, gf, gw, gq_out, gk_out, gv_out, gf_out, gw_out, sem):
    copies = [
        pltpu.make_async_copy(src.at[pl.ds(r * 256, 256)], dst.at[pl.ds(r * 256, 256)], sem.at[i, r])
        for r in range(4)
        for i, (src, dst) in enumerate(((gq, gq_out), (gk, gk_out), (gv, gv_out)))
    ]
    for c in copies:
        c.start()
    gw_out[...] = gw[...].T
    gf_out[...] = gf[:, :64]
    for c in copies:
        c.wait()


def shards(queries, keys, values, filters, grad_out, out_weight):
    hbm = pl.BlockSpec(memory_space=pl.ANY)
    vm = pltpu.VMEM
    out = pl.pallas_call(
        kernel,
        out_shape=(
            vm((TOK, CH), BF16),
            vm((TOK, CH), BF16),
            vm((TOK, CH), BF16),
            vm((8, 128), F32),
            vm((CH, OWN), BF16),
        ),
        in_specs=[hbm, hbm, hbm, pl.BlockSpec(memory_space=pltpu.VMEM), hbm, hbm],
        out_specs=(pl.BlockSpec(memory_space=pltpu.VMEM),) * 5,
        scratch_shapes=[
            vm((TOK, CH), BF16),
            vm((TOK + FILT, CH), BF16),
            vm((TOK + FILT, CH), BF16),
            vm((CH, TOK), BF16),
            vm((8, TOK, EB), BF16),
            vm((4096, CH), BF16),
            vm((16, CH, OWN), BF16),
            vm((10, 6, max(QUART), OWN), BF16),
            vm((1024, 256), BF16),
            vm((64, 256), F32),
            vm((64, 256), F32),
            vm((128, 256), F32),
            vm((4, 4, 8, 128), F32),
            vm((3, 4, 8, 128), F32),
            vm((4, 8, 128), F32),
            vm((3, 8, 128), F32),
            pltpu.SemaphoreType.DMA((COPIES,)),
            pltpu.SemaphoreType.DMA((COPIES,)),
            pltpu.SemaphoreType.DMA((7,)),
        ],
        compiler_params=pltpu.CompilerParams(
            collective_id=0, has_side_effects=True, vmem_limit_bytes=53 * 1024 * 1024
        ),
        name="hyena_bwd",
    )(queries, keys, values, filters, grad_out, out_weight)
    gq, gk, gv, gf, gw = pl.pallas_call(
        store,
        out_shape=(
            jax.ShapeDtypeStruct((TOK, CH), BF16),
            jax.ShapeDtypeStruct((TOK, CH), BF16),
            jax.ShapeDtypeStruct((TOK, CH), BF16),
            jax.ShapeDtypeStruct((8, 64), F32),
            jax.ShapeDtypeStruct((OWN, CH), BF16),
        ),
        in_specs=[hbm] * 3 + [pl.BlockSpec(memory_space=vm)] * 2,
        out_specs=(hbm,) * 3 + (pl.BlockSpec(memory_space=vm),) * 2,
        scratch_shapes=[pltpu.SemaphoreType.DMA((3, 4))],
        compiler_params=pltpu.CompilerParams(vmem_limit_bytes=4 * 1024 * 1024),
        name="store",
    )(*out)
    return gq, gk, gv, gf.T, gw


def solution(mesh):
    return jax.shard_map(
        shards,
        mesh=mesh,
        in_specs=(
            P("seq", "ch"),
            P("seq", "ch"),
            P("seq", "ch"),
            P("ch", None),
            P("seq", "ch"),
            P("seq", "ch"),
        ),
        out_specs=(P("seq", "ch"), P("seq", "ch"), P("seq", "ch"), P("ch", "seq"), P("seq", "ch")),
        check_vma=False,
    )
```

```python
import jax
import jax.numpy as jnp
from jax import lax
from jax.experimental import pallas as pl
from jax.experimental.pallas import tpu as pltpu
from jax.sharding import PartitionSpec as P

F32 = jnp.float32
BF16 = jnp.bfloat16
MESH = pl.DeviceIdType.MESH
FILT = 128
TOK = 1024
CH = 1024
OWN = 256
EB = 512
SPLIT = (0, 448)
QUART = (224, 288)

W_COPIES, A_COPIES, R_COPIES = 36, 13, 60
A_BASE = W_COPIES
R_BASE = A_BASE + A_COPIES
H_BASE = R_BASE + R_COPIES
F_BASE = H_BASE + 2
COPIES = F_BASE + 6


def kernel(
    q_hbm, k_hbm, v_hbm, f_ref, a_hbm, w_hbm,
    mx, kb, vb, gfo, gwo,
    qb, pe, ge, gt, afull, wfull, part,
    boxes, tbl, rback, rahead, gfr, g1, r1, g2, r2,
    ssem, rsem, lsem,
):
    s = lax.axis_index("seq")
    h = lax.axis_index("ch")
    y, z = s // 4, s % 4
    xx, core = h // 2, h % 2

    def at(c, by):
        return (c + by + 4) % 4

    def dev_y(by):
        return (at(y, by) * 4 + z, h)

    def dev_z(by):
        return (y * 4 + at(z, by), h)

    def dev_x(by):
        return (s, at(xx, by) * 2 + core)

    sibling = (s, xx * 2 + (1 - core))
    after = ((s + 1) % 16, h)
    before = ((s + 15) % 16, h)

    sent = []

    def send(src, dst, k, dev):
        c = pltpu.make_async_remote_copy(
            src_ref=src, dst_ref=dst, send_sem=ssem.at[k], recv_sem=rsem.at[k],
            device_id=dev, device_id_type=MESH,
        )
        c.start()
        sent.append(c)

    def arrived(dst, k):
        pltpu.make_async_remote_copy(
            src_ref=dst, dst_ref=dst, send_sem=ssem.at[k], recv_sem=rsem.at[k],
            device_id=sibling, device_id_type=MESH,
        ).wait_recv()

    def local(src, dst, k):
        c = pltpu.make_async_copy(src, dst, lsem.at[k])
        c.start()
        return c

    peers = [dev_y(1), dev_y(2), dev_y(3), dev_z(1), dev_z(2), dev_z(3), dev_x(1), dev_x(3), sibling, after, before]
    bar = pltpu.get_barrier_semaphore()
    for p in peers:
        pl.semaphore_signal(bar, inc=1, device_id=p, device_id_type=MESH)

    own_w = wfull.at[pl.ds(pl.multiple_of(s * OWN, OWN), OWN)]
    tail, rest = pl.ds(TOK - FILT, FILT), pl.ds(0, TOK - FILT)
    ld_tail = [local(k_hbm.at[tail], kb.at[tail], 0), local(v_hbm.at[tail], vb.at[tail], 1)]
    ld_rest = [local(k_hbm.at[rest], kb.at[rest], 2), local(v_hbm.at[rest], vb.at[rest], 3)]
    ld_q = local(q_hbm, qb, 4)
    ld_w = local(w_hbm, own_w, 5)
    ld_a = local(a_hbm, afull.at[h], 6)

    def product_rows(r):
        rows = pl.ds(r, 128)
        pe[pl.ds(r + FILT, 128)] = (kb[rows].astype(F32) * vb[rows].astype(F32)).astype(BF16)

    pl.semaphore_wait(bar, len(peers))

    def wrows(yy, zz, start, size):
        return wfull.at[pl.ds(pl.multiple_of((yy * 4 + zz) * OWN + start, 64), size)]

    own_first = wrows(y, z, 0, 128)
    own_second = wrows(y, z, 128, 128)
    first_rows, second_rows = w_hbm.at[pl.ds(0, 128)], w_hbm.at[pl.ds(128, 128)]
    send(first_rows, own_first, 0, dev_z(1))
    send(first_rows, own_first, 1, dev_z(-1))
    send(first_rows, own_first, 2, dev_y(1))
    send(second_rows, own_second, 3, dev_y(-1))
    send(second_rows, own_second, 33, dev_z(-1))
    send(second_rows, own_second, 34, dev_y(1))
    send(first_rows, own_first, 35, dev_y(-1))

    def ablk(bx, bc, half=None):
        r = afull.at[at(xx, bx) * 2 + bc]
        return r if half is None else r.at[pl.ds(half * 512, 512)]

    own_lo, own_hi = ablk(0, core, 0), ablk(0, core, 1)
    send(a_hbm.at[pl.ds(0, 512)], own_lo, A_BASE + 0, dev_x(1))
    send(a_hbm.at[pl.ds(512, 512)], own_hi, A_BASE + 1, dev_x(-1))
    send(a_hbm.at[pl.ds(512, 512)], own_hi, A_BASE + 2, dev_x(1))
    send(a_hbm.at[pl.ds(0, 512)], own_lo, A_BASE + 3, dev_x(-1))
    send(a_hbm, ablk(0, core), A_BASE + 4, sibling)

    def w1_z_minus():
        r = wrows(y, at(z, -1), 0, 128)
        arrived(r, 0)
        send(r, r, 4, dev_z(1))
        send(r, r, 8, dev_y(1))
        send(r, r, 9, dev_y(-1))

    def w1_z_plus():
        r = wrows(y, at(z, 1), 0, 128)
        arrived(r, 1)
        send(r, r, 10, dev_y(1))
        send(r, r, 11, dev_y(-1))

    def w1_z_plus_second():
        r = wrows(y, at(z, 1), 128, 128)
        arrived(r, 33)
        send(r, r, 5, dev_z(-1))

    def w1_y_minus():
        r = wrows(at(y, -1), z, 0, 128)
        arrived(r, 2)
        send(r, r, 6, dev_y(1))

    def w1_y_minus_second():
        r = wrows(at(y, -1), z, 128, 128)
        arrived(r, 34)
        send(r, r, 14, dev_z(1))
        send(r, r, 15, dev_z(-1))

    def w1_y_plus():
        r = wrows(at(y, 1), z, 128, 128)
        arrived(r, 3)
        send(r, r, 7, dev_y(-1))
        send(r, r, 16, dev_z(1))
        send(r, r, 17, dev_z(-1))

    def w2_z():
        r = wrows(y, at(z, 2), 0, 128)
        arrived(r, 4)
        send(r, r, 12, dev_y(1))
        send(r, r, 13, dev_y(-1))

    def w2_y():
        r = wrows(at(y, 2), z, 128, 128)
        arrived(r, 7)
        send(r, r, 18, dev_z(1))
        send(r, r, 19, dev_z(-1))

    def w3(i, piece):
        bz = (-1, 1, 2)[i]
        if piece == 0:
            r = wrows(at(y, -1), at(z, bz), 0, 128)
            arrived(r, 8 + 2 * i)
            r = wrows(at(y, -1), at(z, bz), 0, 64)
            send(r, r, 20 + 2 * i, dev_y(1))
        elif piece == 1:
            r = wrows(at(y, 1), at(z, bz), 0, 128)
            arrived(r, 9 + 2 * i)
            r = wrows(at(y, 1), at(z, bz), 64, 64)
            send(r, r, 21 + 2 * i, dev_y(-1))
        elif piece == 2:
            r = wrows(at(y, bz), at(z, -1), 128, 128)
            arrived(r, 14 + 2 * i)
            r = wrows(at(y, bz), at(z, -1), 128, 64)
            send(r, r, 26 + 2 * i, dev_z(1))
        else:
            r = wrows(at(y, bz), at(z, 1), 128, 128)
            arrived(r, 15 + 2 * i)
            r = wrows(at(y, bz), at(z, 1), 192, 64)
            send(r, r, 27 + 2 * i, dev_z(-1))

    def w_last():
        arrived(wrows(y, at(z, -1), 128, 128), 32)
        arrived(wrows(at(y, 1), z, 0, 128), 35)
        arrived(wrows(y, at(z, 2), 128, 128), 5)
        arrived(wrows(at(y, 2), z, 0, 128), 6)
        for i in range(3):
            bz = (-1, 1, 2)[i]
            arrived(wrows(at(y, 2), at(z, bz), 0, 64), 20 + 2 * i)
            arrived(wrows(at(y, 2), at(z, bz), 64, 64), 21 + 2 * i)
            arrived(wrows(at(y, bz), at(z, 2), 128, 64), 26 + 2 * i)
            arrived(wrows(at(y, bz), at(z, 2), 192, 64), 27 + 2 * i)

    def near(bx, half, k):
        r = ablk(bx, core, half)
        arrived(r, A_BASE + k)
        if k < 2:
            send(r, r, A_BASE + 5 + k, dev_x(-bx))
        send(r, r, A_BASE + 7 + (0, 1, 2, 3)[k], sibling)

    def far(half):
        r = ablk(2, core, half)
        arrived(r, A_BASE + 5 + half)
        send(r, r, A_BASE + 11 + half, sibling)

    def from_sibling(bx):
        if bx == 0:
            arrived(ablk(0, 1 - core), A_BASE + 4)
            return
        lo, hi = {-1: (7, 9), 1: (10, 8), 2: (11, 12)}[bx]
        arrived(ablk(bx, 1 - core, 0), A_BASE + lo)
        arrived(ablk(bx, 1 - core, 1), A_BASE + hi)

    def rs(hf, stage, i):
        along_z = (hf == 0) == (stage == 0)
        other = at(y if along_z else z, i)
        dev = dev_z if along_z else dev_y
        slot = hf * 5 + (i if stage == 0 else 4)
        base = R_BASE + slot * 6
        size = QUART[hf]

        def chunk(by, q):
            idx = other * 4 + at(z, by) if along_z else at(y, by) * 4 + other
            return part.at[idx, pl.ds(SPLIT[hf] + q * size, size)]

        def box(kind, q):
            return boxes.at[slot, kind * 2 + q, pl.ds(0, size)]

        def direct(q):
            by = (-1, 1)[q]
            send(chunk(by, 1 - q), box(1, q), base + 2 + q, dev(by))

        def start():
            send(chunk(2, 0), box(0, 0), base + 0, dev(-1))
            send(chunk(2, 1), box(0, 1), base + 1, dev(1))
            if stage == 0:
                direct(0)
                direct(1)

        def mid(q):
            by = (-1, 1)[q]
            arrived(box(0, q), base + q)
            c = chunk(by, q)
            c[...] = (c[...].astype(F32) + box(0, q)[...].astype(F32)).astype(BF16)
            send(c, box(2, q), base + 4 + q, dev(by))

        def fin():
            for kind in (1, 2):
                for q in (0, 1):
                    arrived(box(kind, q), base + 2 * kind + q)
            for q in (0, 1):
                c = chunk(0, q)
                total = c[...].astype(F32) + box(1, 1 - q)[...].astype(F32) + box(2, q)[...].astype(F32)
                if stage == 0:
                    c[...] = total.astype(BF16)
                else:
                    gwo[SPLIT[hf] + q * size : SPLIT[hf] + (q + 1) * size] = total.astype(BF16)

        return start, mid, fin, direct

    for c in ld_tail:
        c.wait()
    product_rows(TOK - FILT)
    send(pe.at[pl.ds(TOK, FILT)], pe.at[pl.ds(0, FILT)], H_BASE, after)
    send(second_rows, own_second, 32, dev_z(1))
    for c in ld_rest:
        c.wait()

    def product_loop(i, _):
        product_rows(pl.multiple_of(i * 128, 128))
        return 0

    lax.fori_loop(0, TOK // 128 - 1, product_loop, 0)

    tap = lax.broadcasted_iota(jnp.int32, (FILT, 256), 0)
    lane = lax.broadcasted_iota(jnp.int32, (FILT, 256), 1)
    f = f_ref[...]
    rback[...] = jnp.dot(f, (lane == FILT - tap).astype(F32).astype(BF16), preferred_element_type=F32)
    rahead[...] = jnp.dot(f, (lane == tap).astype(F32).astype(BF16), preferred_element_type=F32)
    group_of = (lane % 128) // 16

    def lanes_of(L):
        return pl.ds(pl.multiple_of(L * 128, 128), 128)

    def make_table(rows_ref, L):
        rows = rows_ref[pl.ds(pl.multiple_of(L * 8, 8), 8), :]
        for g in range(8):
            wide = jnp.broadcast_to(rows[g : g + 1, :], (FILT, 256))
            tbl[g * FILT : (g + 1) * FILT, :] = pltpu.roll(wide, 0, 1, stride=1, stride_axis=0).astype(BF16)

    def windows(ref, p, lanes):
        return jnp.concatenate([ref[pl.ds(p * 256, 256), lanes], ref[pl.ds(p * 256 + 128, 256), lanes]], axis=1)

    def filtered(ref, p, lanes):
        res = jnp.dot(tbl[...], windows(ref, p, lanes), preferred_element_type=F32)
        out = res[0:FILT]
        for g in range(1, 8):
            out = jnp.where(group_of == g, res[g * FILT : (g + 1) * FILT], out)
        return jnp.concatenate([out[:, :128], out[:, 128:]], axis=0)

    def conv_mixed(L, _):
        lanes = lanes_of(L)
        make_table(rback, L)
        for p in range(4):
            m = filtered(pe, p, lanes)
            rows = pl.ds(p * 256, 256)
            mx[rows, lanes] = m.astype(BF16)
            gated = (qb[rows, lanes].astype(F32) * m).astype(BF16)
            gt[lanes, rows] = gated.T
        return 0

    def prior_product():
        arrived(pe.at[pl.ds(0, FILT)], H_BASE)

        @pl.when(s == 0)
        def _():
            pe[pl.ds(0, FILT)] = jnp.zeros((FILT, CH), BF16)

        ld_q.wait()

    def weight_grad(bx, bc):
        blk = at(xx, bx) * 2 + bc

        def one(u, _):
            cols = pl.ds(pl.multiple_of(u * 256, 256), 256)
            r = jnp.dot(gt[...], afull[blk, :, cols], preferred_element_type=F32)
            part[blk * 2 + u] = r.astype(BF16)
            return 0

        lax.fori_loop(0, 2, one, 0)

    def rs_x(bx):
        return rs(0, 0, (xx + bx - y + 8) % 4)

    start, mid, fin, direct = 0, 1, 2, 3

    def gated_grad(n, _):
        cols = pl.ds(pl.multiple_of(n * 256, 256), 256)
        acc = jnp.dot(afull[0], wfull[pl.ds(0, EB), cols], preferred_element_type=F32)
        for b in range(1, 8):
            acc = acc + jnp.dot(afull[b], wfull[pl.ds(b * EB, EB), cols], preferred_element_type=F32)
        gg = acc.astype(BF16).astype(F32)
        ge[pl.ds(0, TOK), cols] = (gg * qb[:, cols].astype(F32)).astype(BF16)
        mx[:, cols] = (gg * mx[:, cols].astype(F32)).astype(BF16)
        return 0

    def send_mixed_halo():
        send(ge.at[pl.ds(0, FILT)], ge.at[pl.ds(TOK, FILT)], H_BASE + 1, before)

    flip = (lax.broadcasted_iota(jnp.int32, (FILT, FILT), 0) + lax.broadcasted_iota(jnp.int32, (FILT, FILT), 1) == FILT - 1)
    flip = flip.astype(F32).astype(BF16)

    def lag_products(L, _):
        lanes = lanes_of(L)
        acc = None
        for p in range(4):
            own = jnp.concatenate([ge[pl.ds(p * 256, 128), lanes], ge[pl.ds(p * 256 + 128, 128), lanes]], axis=1)
            own = jnp.dot(flip, own, preferred_element_type=F32)
            lhs = jnp.concatenate([jnp.where(group_of == g, own, 0.0).astype(BF16) for g in range(8)], axis=0)
            d = lax.dot_general(lhs, windows(pe, p, lanes), (((1,), (1,)), ((), ())), preferred_element_type=F32)
            acc = d if acc is None else acc + d
        sums = []
        for g in range(8):
            skew = pltpu.roll(acc[g * FILT : (g + 1) * FILT], 0, 1, stride=1, stride_axis=0)
            sums.append(jnp.sum(skew, axis=0, keepdims=True))
        gfr[pl.ds(pl.multiple_of(L * 8, 8), 8), :] = jnp.concatenate(sums, axis=0)
        return 0

    def send_taps_z():
        pick = (lane == 255 - tap).astype(F32).astype(BF16)
        hi = gfr[...].astype(BF16)
        lo = (gfr[...] - hi.astype(F32)).astype(BF16)
        nt = (((1,), (1,)), ((), ()))
        taps = lax.dot_general(pick, hi, nt, preferred_element_type=F32)
        taps = taps + lax.dot_general(pick, lo, nt, preferred_element_type=F32)
        for i in range(16):
            g1[i % 4, i // 4] = taps[i * 8 : (i + 1) * 8]
        for d in (1, 2, 3):
            send(g1.at[at(z, d)], r1.at[d - 1], F_BASE + d - 1, dev_z(d))

    def send_taps_y():
        for d in (1, 2, 3):
            arrived(r1.at[d - 1], F_BASE + d - 1)
        g2[...] = g1[z] + r1[0] + r1[1] + r1[2]
        for d in (1, 2, 3):
            send(g2.at[at(y, d)], r2.at[d - 1], F_BASE + 2 + d, dev_y(d))

    def sum_taps():
        for d in (1, 2, 3):
            arrived(r2.at[d - 1], F_BASE + 2 + d)
        gfo[...] = g2[y] + r2[0] + r2[1] + r2[2]

    def later_mixed():
        arrived(ge.at[pl.ds(TOK, FILT)], H_BASE + 1)

        @pl.when(s == 15)
        def _():
            ge[pl.ds(TOK, FILT)] = jnp.zeros((FILT, CH), BF16)

    def conv_grad(L, _):
        lanes = lanes_of(L)
        make_table(rahead, L)
        for p in range(4):
            m = filtered(ge, p, lanes)
            rows = pl.ds(p * 256, 256)
            keys, values = kb[rows, lanes].astype(F32), vb[rows, lanes].astype(F32)
            kb[rows, lanes] = (m * values).astype(BF16)
            vb[rows, lanes] = (m * keys).astype(BF16)
        return 0

    ld_w.wait()
    w1_z_minus()
    w1_y_plus()
    prior_product()
    lax.fori_loop(0, 1, conv_mixed, 0)
    w1_y_minus()
    lax.fori_loop(1, 2, conv_mixed, 0)
    near(-1, 0, 0)
    w1_z_plus_second()
    near(1, 1, 1)
    w1_z_plus()
    lax.fori_loop(2, 3, conv_mixed, 0)
    w1_y_minus_second()
    w3(0, 0)
    lax.fori_loop(3, 6, conv_mixed, 0)
    w2_z()
    lax.fori_loop(6, 7, conv_mixed, 0)
    w2_y()
    near(1, 0, 3)
    near(-1, 1, 2)
    lax.fori_loop(7, 8, conv_mixed, 0)
    ld_a.wait()
    weight_grad(0, core)
    from_sibling(0)
    weight_grad(0, 1 - core)
    from_sibling(1)
    weight_grad(1, 1 - core)
    w3(1, 2)
    w3(1, 3)
    weight_grad(1, core)
    w3(0, 3)
    w3(1, 1)
    w3(0, 1)
    w3(1, 0)
    far(1)
    from_sibling(-1)
    weight_grad(-1, 1 - core)
    far(0)
    weight_grad(-1, core)
    w3(2, 3)
    w3(0, 2)
    w3(2, 1)
    weight_grad(2, core)
    w3(2, 0)
    w3(2, 2)
    rs_x(0)[start]()
    rs_x(-1)[start]()
    from_sibling(2)
    weight_grad(2, 1 - core)
    rs(1, 0, 2)[start]()
    rs_x(2)[start]()
    rs(1, 0, 2)[mid](0)
    rs(1, 0, 1)[start]()
    rs(1, 0, 2)[mid](1)
    w_last()
    rs_x(1)[start]()
    lax.fori_loop(0, 1, gated_grad, 0)
    rs_x(0)[mid](1)
    rs(1, 0, 3)[start]()
    lax.fori_loop(1, 4, gated_grad, 0)
    send_mixed_halo()
    gfr[...] = jnp.zeros((128, 256), F32)
    lax.fori_loop(0, 1, lag_products, 0)
    rs(1, 0, 1)[mid](1)
    rs_x(0)[mid](0)
    lax.fori_loop(1, 2, lag_products, 0)
    rs_x(-1)[mid](1)
    lax.fori_loop(2, 3, lag_products, 0)
    rs(1, 0, 2)[fin]()
    rs(1, 0, 1)[mid](0)
    rs_x(2)[mid](1)
    rs_x(1)[mid](0)
    rs(1, 0, 0)[start]()
    lax.fori_loop(3, 4, lag_products, 0)
    rs_x(1)[mid](1)
    lax.fori_loop(4, 6, lag_products, 0)
    rs_x(2)[mid](0)
    lax.fori_loop(6, 7, lag_products, 0)
    rs(1, 0, 3)[mid](0)
    later_mixed()
    lax.fori_loop(0, 1, conv_grad, 0)
    rs_x(-1)[mid](0)
    lax.fori_loop(1, 2, conv_grad, 0)
    lax.fori_loop(7, 8, lag_products, 0)
    rs(1, 0, 3)[mid](1)
    rs(1, 0, 1)[fin]()
    send_taps_z()
    rs(1, 0, 0)[mid](0)
    lax.fori_loop(2, 3, conv_grad, 0)
    rs(1, 1, 0)[start]()
    rs(1, 0, 0)[mid](1)
    rs(1, 1, 0)[direct](1)
    lax.fori_loop(3, 4, conv_grad, 0)
    rs(0, 0, 2)[fin]()
    rs(0, 1, 0)[start]()
    rs(0, 0, 3)[fin]()
    rs(1, 0, 3)[fin]()
    rs(0, 1, 0)[direct](0)
    rs(1, 1, 0)[direct](0)
    rs(0, 0, 1)[fin]()
    rs(0, 1, 0)[direct](1)
    lax.fori_loop(4, 6, conv_grad, 0)
    rs(1, 1, 0)[mid](1)
    send_taps_y()
    rs(1, 1, 0)[mid](0)
    rs(0, 1, 0)[mid](1)
    rs(0, 1, 0)[mid](0)
    rs(1, 0, 0)[fin]()
    lax.fori_loop(6, 8, conv_grad, 0)
    rs(0, 0, 0)[fin]()
    sum_taps()
    rs(1, 1, 0)[fin]()
    rs(0, 1, 0)[fin]()
    for c in sent:
        c.wait_send()


def store(gq, gk, gv, gf, gw, gq_out, gk_out, gv_out, gf_out, gw_out, sem):
    copies = [
        pltpu.make_async_copy(src.at[pl.ds(r * 256, 256)], dst.at[pl.ds(r * 256, 256)], sem.at[i, r])
        for r in range(4)
        for i, (src, dst) in enumerate(((gq, gq_out), (gk, gk_out), (gv, gv_out)))
    ]
    for c in copies:
        c.start()
    gw_out[...] = gw[...].T
    gf_out[...] = gf[:, :64]
    for c in copies:
        c.wait()


def shards(queries, keys, values, filters, grad_out, out_weight):
    hbm = pl.BlockSpec(memory_space=pl.ANY)
    vm = pltpu.VMEM
    out = pl.pallas_call(
        kernel,
        out_shape=(
            vm((TOK, CH), BF16),
            vm((TOK, CH), BF16),
            vm((TOK, CH), BF16),
            vm((8, 128), F32),
            vm((CH, OWN), BF16),
        ),
        in_specs=[hbm, hbm, hbm, pl.BlockSpec(memory_space=pltpu.VMEM), hbm, hbm],
        out_specs=(pl.BlockSpec(memory_space=pltpu.VMEM),) * 5,
        scratch_shapes=[
            vm((TOK, CH), BF16),
            vm((TOK + FILT, CH), BF16),
            vm((TOK + FILT, CH), BF16),
            vm((CH, TOK), BF16),
            vm((8, TOK, EB), BF16),
            vm((4096, CH), BF16),
            vm((16, CH, OWN), BF16),
            vm((10, 6, max(QUART), OWN), BF16),
            vm((1024, 256), BF16),
            vm((64, 256), F32),
            vm((64, 256), F32),
            vm((128, 256), F32),
            vm((4, 4, 8, 128), F32),
            vm((3, 4, 8, 128), F32),
            vm((4, 8, 128), F32),
            vm((3, 8, 128), F32),
            pltpu.SemaphoreType.DMA((COPIES,)),
            pltpu.SemaphoreType.DMA((COPIES,)),
            pltpu.SemaphoreType.DMA((7,)),
        ],
        compiler_params=pltpu.CompilerParams(
            collective_id=0, has_side_effects=True, vmem_limit_bytes=53 * 1024 * 1024
        ),
        name="hyena_bwd",
    )(queries, keys, values, filters, grad_out, out_weight)
    gq, gk, gv, gf, gw = pl.pallas_call(
        store,
        out_shape=(
            jax.ShapeDtypeStruct((TOK, CH), BF16),
            jax.ShapeDtypeStruct((TOK, CH), BF16),
            jax.ShapeDtypeStruct((TOK, CH), BF16),
            jax.ShapeDtypeStruct((8, 64), F32),
            jax.ShapeDtypeStruct((OWN, CH), BF16),
        ),
        in_specs=[hbm] * 3 + [pl.BlockSpec(memory_space=vm)] * 2,
        out_specs=(hbm,) * 3 + (pl.BlockSpec(memory_space=vm),) * 2,
        scratch_shapes=[pltpu.SemaphoreType.DMA((3, 4))],
        compiler_params=pltpu.CompilerParams(vmem_limit_bytes=4 * 1024 * 1024),
        name="store",
    )(*out)
    return gq, gk, gv, gf.T, gw


def solution(mesh):
    return jax.shard_map(
        shards,
        mesh=mesh,
        in_specs=(
            P("seq", "ch"),
            P("seq", "ch"),
            P("seq", "ch"),
            P("ch", None),
            P("seq", "ch"),
            P("seq", "ch"),
        ),
        out_specs=(P("seq", "ch"), P("seq", "ch"), P("seq", "ch"), P("ch", "seq"), P("seq", "ch")),
        check_vma=False,
    )
```
